128 devices in a mesh: rows: 64 (over z, x, y), rep: 2 (over core).
Axes of the slice: x: 4, y: 4, z: 4, core: 2. Of those that a mesh axis runs over, the one named last changes fastest.
Arguments:
- node_feats: bfloat16 [131072, 128], P('rows'), may hold values from -6 to 6
- w_in: bfloat16 [128, 256], replicated, may hold values from -0.5 to 0.5
- w_out: bfloat16 [256, 172], replicated
- labels: int32 [131072], P(('rows', 'rep')), may hold values from 0 to 171
- hub_rows: int32 [64, 2, 64], P('rows', 'rep'), may hold values from 0 to 2047, as said below
- send_rows: int32 [64, 2, 512], P('rows', 'rep'), may hold values from -1 to 2047, as said below
- adj_hub: bfloat16 [131072, 2, 4096], P('rows', 'rep'), may hold values from -0.0625 to 0.0625
- adj_sparse: bfloat16 [131072, 2, 512], P('rows', 'rep'), may hold values from -0.1875 to 0.1875
Outputs:
- logits: bfloat16 [131072, 172], P(('rows', 'rep'))
- grad_in: float32 [128, 256], replicated
- grad_out: float32 [256, 172], replicated
The draws below stay inside these ranges and needn't reach their ends.
Inputs may be any that keep to these rules, and one draw needn't show every extreme that they name: `hub_rows`: within each owner slab the 2 x 64 hub nodes are distinct. `send_rows`: for each source, half and destination the live slots (not -1) come first; their count is 1 to 8, and for every source and half some destination has all 8 slots live. A node may fill several slots.
All inputs are finite; a program needn't handle non-finite values.
Results may differ from the reference program's by a relative error of at most 0.0095.
The reference program's roundings to bfloat16 on the way (of `first`, `hidden` and `second`) count: a program that leaves them out, or rounds other values in their place, can miss the bound.
Values may be sent and summed in bfloat16 or wider, within the bound.
No kernel may reach another device: no remote copies, remote signals or barrier semaphores. Data moves between devices by JAX's collectives and lax.ppermute only.
A program may use at most 128 MiB of HBM per device.

```python
import jax
import jax.numpy as jnp
from jax import lax

F = 128
HID = 256
C = 172
ROWS_DEV = 2048
HUBH = 64
CAPH = 8
NODES = 131072
HUB_ALL = 8192
SLOT_ALL = 1024
N_ROWS = 64
N_REP = 2


def draw_w_out(key, part):
    base = jax.random.normal(key, (HID, C), jnp.float32) * HID ** (-0.5)
    return base.astype(jnp.bfloat16)


def draw_hub_rows(key, part):
    keys = jax.random.split(jax.random.fold_in(key, 21), N_ROWS)
    perms = jax.vmap(lambda single: jax.random.permutation(single, ROWS_DEV))(keys)
    return perms[:, :N_REP * HUBH].reshape(N_ROWS, N_REP, HUBH).astype(jnp.int32)


def draw_send_rows(key, part):
    key_count = jax.random.fold_in(key, 31)
    key_full = jax.random.fold_in(key, 32)
    key_rows = jax.random.fold_in(key, 33)
    counts = jax.random.randint(key_count, (N_ROWS, N_REP, N_ROWS), 1, CAPH + 1)
    full = jax.random.randint(key_full, (N_ROWS, N_REP, 1), 0, N_ROWS)
    counts = jnp.where(jnp.arange(N_ROWS)[None, None, :] == full, CAPH, counts)
    rows = jax.random.randint(key_rows, (N_ROWS, N_REP, N_ROWS, CAPH), 0, ROWS_DEV)
    live = jnp.arange(CAPH)[None, None, None, :] < counts[..., None]
    return jnp.where(live, rows, -1).reshape(N_ROWS, N_REP, N_ROWS * CAPH).astype(jnp.int32)


def touch_ends(drawn, stream_key, low, top_value):
    spot = [jax.random.randint(jax.random.fold_in(stream_key, axis), (), 0, length) for axis, length in enumerate(drawn.shape)]
    widest = drawn.shape.index(max(drawn.shape))
    beside = spot[:widest] + [(spot[widest] + 1) % drawn.shape[widest]] + spot[widest + 1:]
    return drawn.at[tuple(spot)].set(low).at[tuple(beside)].set(top_value)


def shard_levels(rng, shape, pieces, low, largest):
    loudness, own = 1.0, jax.random.fold_in(rng, 6)
    for dim, blocks in pieces:
        heights = jnp.exp(jax.random.uniform(jax.random.fold_in(own, dim), (blocks,), jnp.float32, low / len(pieces), largest / len(pieces)))
        loudness = loudness * jnp.repeat(heights, shape[dim] // blocks).reshape([-1 if axis == dim else 1 for axis in range(len(shape))])
    return loudness


def noise(stream_key, dims, scale, reach, shards=(), kind=jnp.bfloat16):
    drawn = jax.random.normal(stream_key, dims, jnp.float32) * scale
    if len(shards) > 0:
        drawn = shard_levels(stream_key, dims, shards, -0.22, 0.18) * drawn
    return jnp.clip(drawn, min=-reach, max=reach).astype(kind)


def setup_inputs(seed: int = 0) -> dict:
    arg_keys = jax.random.split(jax.random.key(seed), 9)
    return {
        "node_feats": noise(arg_keys[0], (NODES, F), 1.0, 6.0, ((0, 64),)),
        "w_in": noise(arg_keys[1], (F, HID), F ** -0.5, 0.5),
        "w_out": draw_w_out(jax.random.fold_in(arg_keys[8], 71), 0),
        "labels": touch_ends(jax.random.randint(arg_keys[3], (NODES,), 0, C), jax.random.fold_in(arg_keys[3], 1), 0, C - 1).astype(jnp.int32),
        "hub_rows": draw_hub_rows(jax.random.fold_in(arg_keys[8], 71), 0),
        "send_rows": draw_send_rows(jax.random.fold_in(arg_keys[8], 71), 0),
        "adj_hub": noise(arg_keys[6], (NODES, N_REP, N_ROWS * HUBH), HUB_ALL ** -0.5, 0.0625, ((0, 64), (1, 2))),
        "adj_sparse": noise(arg_keys[7], (NODES, N_REP, N_ROWS * CAPH), SLOT_ALL ** -0.5, 0.1875, ((0, 64), (1, 2))),
    }


def hub_node_ids(hub_rows):
    owners = jnp.arange(N_ROWS, dtype=jnp.int32)[:, None, None] * ROWS_DEV
    glob = owners + hub_rows
    return jnp.transpose(glob, (1, 0, 2)).reshape(N_REP, N_ROWS * HUBH)

def slot_node_ids(send_rows, slab):
    block = lax.dynamic_slice_in_dim(send_rows, (slab * CAPH).astype(jnp.int32), CAPH, 2)
    owners = jnp.arange(N_ROWS, dtype=jnp.int32)[:, None, None] * ROWS_DEV
    glob = jnp.transpose(owners + block, (1, 0, 2)).reshape(N_REP, N_ROWS * CAPH)
    live = jnp.transpose(block >= 0, (1, 0, 2)).reshape(N_REP, N_ROWS * CAPH)
    return (glob, live)

def aggregate(values, hub_rows, send_rows, adj_hub, adj_sparse):
    panel = values[hub_node_ids(hub_rows)]

    def one_slab(slab):
        start = (slab * ROWS_DEV).astype(jnp.int32)
        hub_block = lax.dynamic_slice_in_dim(adj_hub, start, ROWS_DEV, 0)
        sparse_block = lax.dynamic_slice_in_dim(adj_sparse, start, ROWS_DEV, 0)
        glob, live = slot_node_ids(send_rows, slab)
        rows = jnp.where(live[..., None], values[jnp.where(live, glob, 0)], jnp.zeros((), values.dtype))
        total = jnp.zeros((ROWS_DEV, values.shape[1]), jnp.float32)
        for member in range(N_REP):
            total = total + jnp.dot(hub_block[:, member, :], panel[member], preferred_element_type=jnp.float32)
            total = total + jnp.dot(sparse_block[:, member, :], rows[member], preferred_element_type=jnp.float32)
        return total
    out = lax.map(one_slab, jnp.arange(N_ROWS, dtype=jnp.int32))
    return out.reshape(NODES, values.shape[1])

def aggregate_t(grads, hub_rows, send_rows, adj_hub, adj_sparse):
    width = grads.shape[1]
    high = lax.Precision.HIGHEST

    def step(carry, slab):
        out, hub_grad = carry
        start = (slab * ROWS_DEV).astype(jnp.int32)
        hub_block = lax.dynamic_slice_in_dim(adj_hub, start, ROWS_DEV, 0).astype(jnp.float32)
        sparse_block = lax.dynamic_slice_in_dim(adj_sparse, start, ROWS_DEV, 0).astype(jnp.float32)
        local = lax.dynamic_slice_in_dim(grads, start, ROWS_DEV, 0)
        hub_terms = jnp.stack([jnp.dot(hub_block[:, member, :].T, local, precision=high) for member in range(N_REP)])
        slot_terms = jnp.stack([jnp.dot(sparse_block[:, member, :].T, local, precision=high) for member in range(N_REP)])
        glob, live = slot_node_ids(send_rows, slab)
        target = jnp.where(live, glob, NODES).reshape(-1)
        out = out.at[target].add(slot_terms.reshape(-1, width), mode='drop')
        return ((out, hub_grad + hub_terms), None)
    init = (jnp.zeros((NODES, width), jnp.float32), jnp.zeros((N_REP, N_ROWS * HUBH, width), jnp.float32))
    (out, hub_grad), _ = lax.scan(step, init, jnp.arange(N_ROWS, dtype=jnp.int32))
    out = out.at[hub_node_ids(hub_rows).reshape(-1)].add(hub_grad.reshape(-1, width))
    return out

def reference(node_feats, w_in, w_out, labels, hub_rows, send_rows, adj_hub, adj_sparse):
    high = lax.Precision.HIGHEST
    first = aggregate(node_feats, hub_rows, send_rows, adj_hub, adj_sparse).astype(jnp.bfloat16)
    pre = jnp.dot(first, w_in, preferred_element_type=jnp.float32)
    hidden = jnp.maximum(pre, 0.0).astype(jnp.bfloat16)
    second = aggregate(hidden, hub_rows, send_rows, adj_hub, adj_sparse).astype(jnp.bfloat16)
    scores = jnp.dot(second, w_out, preferred_element_type=jnp.float32)
    top = lax.optimization_barrier(jnp.max(scores, axis=1, keepdims=True))
    expo = jnp.exp(scores - top)
    probs = expo / lax.optimization_barrier(jnp.sum(expo, axis=1, keepdims=True))
    onehot = (labels[:, None] == jnp.arange(C, dtype=jnp.int32)[None, :]).astype(jnp.float32)
    dscore = (probs - onehot) * (1.0 / jnp.sqrt(jnp.float32(NODES)))
    grad_out = jnp.dot(second.astype(jnp.float32).T, dscore, precision=high)
    back = aggregate_t(dscore, hub_rows, send_rows, adj_hub, adj_sparse)
    dhidden = jnp.dot(back, w_out.astype(jnp.float32).T, precision=high)
    dpre = jnp.where(pre > 0, dhidden, jnp.zeros((), jnp.float32))
    grad_in = jnp.dot(first.astype(jnp.float32).T, dpre, precision=high)
    return (scores.astype(jnp.bfloat16), grad_in, grad_out)
```

```python
import jax
import jax.numpy as jnp
from jax import lax
from jax.sharding import PartitionSpec as P

SWAP = [(0, 1), (1, 0)]


def on_device(node_feats, w_in, w_out, labels, hub_rows, send_rows, adj_hub, adj_sparse):
    f32, bf16 = jnp.float32, jnp.bfloat16
    nrows = lax.axis_size("rows")
    slab = node_feats.shape[0]
    half = slab // lax.axis_size("rep")
    total_nodes = slab * nrows
    hub_local = hub_rows[0, 0]
    slot_local = send_rows[0, 0]
    hub_count = hub_local.shape[0]
    slot_count = slot_local.shape[0] // nrows
    hub_mat = adj_hub[:, 0, :]
    sparse_mat = adj_sparse[:, 0, :]
    core = lax.axis_index("rep")
    own_start = core * half
    oth_start = (1 - core) * half
    iota = jnp.arange(slab, dtype=jnp.int32)
    pick = (jnp.concatenate([hub_local, slot_local])[:, None] == iota[None, :]).astype(bf16)

    def dot(a, b):
        return jnp.dot(a, b, preferred_element_type=f32)

    def gather(values):
        rows = dot(pick, values).astype(bf16)
        width = rows.shape[1]
        hubs = jnp.broadcast_to(rows[:hub_count][None], (nrows, hub_count, width))
        slots = rows[hub_count:].reshape(nrows, slot_count, width)
        got = lax.all_to_all(
            jnp.concatenate([hubs, slots], axis=1), "rows", split_axis=0, concat_axis=0, tiled=True
        )
        return got[:, :hub_count].reshape(-1, width), got[:, hub_count:].reshape(-1, width)

    hub_x, slot_x = gather(node_feats)
    part = dot(hub_mat, hub_x) + dot(sparse_mat, slot_x)
    first = (part + lax.ppermute(part, "rep", SWAP)).astype(bf16)
    hub_f, slot_f = gather(first)
    hub_h = jnp.maximum(dot(hub_f, w_in), 0.0).astype(bf16)
    slot_h = jnp.maximum(dot(slot_f, w_in), 0.0).astype(bf16)
    part2 = dot(hub_mat, hub_h) + dot(sparse_mat, slot_h)
    away = lax.ppermute(lax.dynamic_slice_in_dim(part2, oth_start, half, 0), "rep", SWAP)
    second = (lax.dynamic_slice_in_dim(part2, own_start, half, 0) + away).astype(bf16)
    scores = dot(second, w_out)
    classes = scores.shape[1]
    top = jnp.max(scores, axis=1, keepdims=True)
    expo = jnp.exp(scores - top)
    probs = expo / jnp.sum(expo, axis=1, keepdims=True)
    onehot = (labels[:, None] == jnp.arange(classes, dtype=jnp.int32)[None, :]).astype(f32)
    dscore = (probs - onehot) * (1.0 / jnp.sqrt(f32(total_nodes)))
    high = dscore.astype(bf16)
    low = (dscore - high.astype(f32)).astype(bf16)
    grad_out_t = dot(high.T, second) + dot(low.T, second)
    dsec = dot(high, w_out.T).astype(bf16)
    dsec_away = lax.ppermute(dsec, "rep", SWAP)
    lower = jnp.where(core == 0, dsec, dsec_away)
    upper = jnp.where(core == 0, dsec_away, dsec)
    dfull = jnp.concatenate([lower, upper], axis=0)
    hub_d = jnp.where(hub_h > 0, dot(hub_mat.T, dfull), 0.0).astype(bf16)
    slot_d = jnp.where(slot_h > 0, dot(sparse_mat.T, dfull), 0.0).astype(bf16)
    grad_in = dot(hub_f.T, hub_d) + dot(slot_f.T, slot_d)

    flat = jnp.concatenate([grad_in, grad_out_t], axis=0)
    count, width = flat.shape
    share = -(-count // nrows)
    flat = jnp.pad(flat, ((0, share * nrows - count), (0, 0))).reshape(nrows, share, width)
    mine = lax.all_to_all(flat, "rows", split_axis=0, concat_axis=0, tiled=True).sum(axis=0)
    mine = mine + lax.ppermute(mine, "rep", SWAP)
    whole = lax.all_to_all(
        jnp.broadcast_to(mine[None], (nrows, share, width)), "rows", split_axis=0, concat_axis=0, tiled=True
    ).reshape(nrows * share, width)
    inner = w_in.shape[0]
    return (scores.astype(bf16), whole[:inner], whole[inner:count].T)


def solution(mesh):
    return jax.shard_map(
        on_device,
        mesh=mesh,
        in_specs=(
            P("rows", None),
            P(),
            P(),
            P(("rows", "rep")),
            P("rows", "rep", None),
            P("rows", "rep", None),
            P("rows", "rep", None),
            P("rows", "rep", None),
        ),
        out_specs=(P(("rows", "rep"), None), P(), P()),
        check_vma=False,
    )
```

```python
import functools
import jax
import jax.numpy as jnp
from jax import lax
from jax.experimental import pallas as pl
from jax.experimental.pallas import tpu as pltpu
from jax.sharding import PartitionSpec as P

SWAP = [(0, 1), (1, 0)]
F32, BF16 = jnp.float32, jnp.bfloat16
VM = pl.BlockSpec(memory_space=pltpu.VMEM)
MIB = 1024 * 1024


def dot(a, b):
    return jnp.dot(a, b, preferred_element_type=F32)


def dot_t(a, b):
    return lax.dot_general(a, b, (((1,), (1,)), ((), ())), preferred_element_type=F32)


def call(body, outs, *args, flops=0, traffic=0, scratch=(), limit=16):
    return pl.pallas_call(
        body,
        out_shape=outs,
        in_specs=[VM] * len(args),
        out_specs=jax.tree.map(lambda _: VM, outs),
        scratch_shapes=scratch,
        compiler_params=pltpu.CompilerParams(vmem_limit_bytes=limit * MIB),
        cost_estimate=pl.CostEstimate(flops=flops, bytes_accessed=traffic, transcendentals=0),
    )(*args)


def one_hot(row, slab):
    count = row.shape[1]
    index = jnp.broadcast_to(row, (128, count)).T
    wide = jnp.concatenate([index] * (slab // 128), axis=1)
    return (wide == lax.broadcasted_iota(jnp.int32, (count, slab), 1)).astype(BF16)


def spread(values, hub_ref, slot_ref, out_ref):
    peers, rows, width = out_ref.shape
    hubs = hub_ref.shape[1]
    slab = values.shape[0]
    hub = dot(one_hot(hub_ref[...], slab), values)
    slot = dot(one_hot(slot_ref[...], slab), values)
    whole = jnp.concatenate(
        [
            jnp.broadcast_to(hub[None], (peers, hubs, width)),
            slot.reshape(peers, rows - hubs, width),
        ],
        axis=1,
    )
    out_ref[...] = whole.astype(BF16)


def pick_body(feat_ref, hub_ref, slot_ref, out_ref):
    spread(feat_ref[...], hub_ref, slot_ref, out_ref)


def pick_sum_body(part_ref, away_ref, hub_ref, slot_ref, out_ref):
    spread((part_ref[...] + away_ref[...]).astype(BF16), hub_ref, slot_ref, out_ref)


def split(got_ref, hubs):
    peers, rows, width = got_ref.shape
    hub = got_ref[:, :hubs, :].reshape(peers * hubs, width)
    slot = got_ref[:, hubs:, :].astype(F32).reshape(peers * (rows - hubs), width).astype(BF16)
    return hub, slot


def first_body(hubs, step, got_ref, hub_mat, sparse_mat, part_ref):
    hub, slot = split(got_ref, hubs)

    @pl.loop(0, part_ref.shape[0] // step)
    def _(i):
        at = pl.ds(pl.multiple_of(i * step, step), step)
        part_ref[at, :] = dot(hub_mat[at, :], hub) + dot(sparse_mat[at, :], slot)


def second_body(step, away, hid_hub, hid_slot, hub_mat, sparse_mat, part_ref):
    core = lax.axis_index("rep")
    start = (1 - core if away else core) * part_ref.shape[0]

    @pl.loop(0, part_ref.shape[0] // step)
    def _(i):
        at = pl.ds(pl.multiple_of(i * step, step), step)
        src = pl.ds(pl.multiple_of(start + i * step, step), step)
        part_ref[at, :] = dot(hub_mat[src, :], hid_hub[...]) + dot(sparse_mat[src, :], hid_slot[...])


def hidden_body(hubs, got_ref, w_ref, hub_out, slot_out):
    hub, slot = split(got_ref, hubs)
    hub_out[...] = jnp.maximum(dot(hub, w_ref[...]), 0.0).astype(BF16)
    slot_out[...] = jnp.maximum(dot(slot, w_ref[...]), 0.0).astype(BF16)


def score_body(scale, part_ref, away_ref, w_ref, label_ref, logit_ref, dsec_ref, grad_ref):
    second = (part_ref[...] + away_ref[...]).astype(BF16)
    scores = dot_t(w_ref[...], second)
    logit_ref[...] = scores.astype(BF16)
    top = jnp.max(scores, axis=0, keepdims=True)
    expo = jnp.exp(scores - top)
    probs = expo / jnp.sum(expo, axis=0, keepdims=True)
    hot = label_ref[...] == lax.broadcasted_iota(jnp.int32, scores.shape, 0)
    dscore = (probs - hot.astype(F32)) * scale
    high = dscore.astype(BF16)
    low = (dscore - high.astype(F32)).astype(BF16)
    grad_ref[...] = dot(high, second) + dot(low, second)
    dsec_ref[...] = lax.dot_general(
        w_ref[...], high, (((0,), (0,)), ((), ())), preferred_element_type=F32
    ).astype(BF16)


def back_body(hubs, step, own_ref, oth_ref, got_ref, w_ref, hub_mat, sparse_mat, grad_ref, dsec_ref, acc_ref):
    half = own_ref.shape[1]
    core = lax.axis_index("rep")
    w_t = w_ref[...].astype(F32).T.astype(BF16)
    peers, rows, width = got_ref.shape

    @pl.when(core == 0)
    def _():
        dsec_ref[:, :half] = own_ref[...]
        dsec_ref[:, half:] = oth_ref[...]

    @pl.when(core != 0)
    def _():
        dsec_ref[:, :half] = oth_ref[...]
        dsec_ref[:, half:] = own_ref[...]

    def term(cols, mat):
        hid = dot_t(w_t, cols)
        grad = jnp.where(hid > 0, dot(dsec_ref[...], mat), 0.0).astype(BF16)
        return dot(grad, cols)

    slot = got_ref[:, hubs:, :].astype(F32).reshape(peers * (rows - hubs), width).astype(BF16)
    acc_ref[...] = term(slot, sparse_mat[...])
    group = step // hubs

    @pl.loop(0, hub_mat.shape[1] // step)
    def _(i):
        at = pl.ds(pl.multiple_of(i * step, step), step)
        cols = got_ref[pl.ds(i * group, group), :hubs, :].reshape(step, width)
        acc_ref[...] += term(cols, hub_mat[:, at])

    grad_ref[...] = acc_ref[...].T


def on_device(node_feats, w_in, w_out, labels, hub_rows, send_rows, adj_hub, adj_sparse):
    nrows = lax.axis_size("rows")
    slab, width = node_feats.shape
    half = slab // lax.axis_size("rep")
    hid, classes = w_out.shape
    hubs = hub_rows.shape[2]
    slots = send_rows.shape[2] // nrows
    hub_cols, slot_cols = nrows * hubs, nrows * slots
    hub_row = hub_rows.reshape(1, hubs)
    slot_row = send_rows.reshape(1, slot_cols)
    hub_mat = pltpu.with_memory_space_constraint(adj_hub.reshape(slab, hub_cols), pltpu.VMEM)
    sparse_mat = pltpu.with_memory_space_constraint(adj_sparse.reshape(slab, slot_cols), pltpu.VMEM)
    shape = jax.ShapeDtypeStruct
    packet = shape((nrows, hubs + slots, width), BF16)
    products = 2 * slab * (hub_cols + slot_cols)

    def exchange(x):
        return lax.all_to_all(x, "rows", split_axis=0, concat_axis=0, tiled=True)

    def swap(x):
        return lax.ppermute(x, "rep", SWAP)

    got = exchange(call(pick_body, packet, node_feats, hub_row, slot_row, traffic=64 * MIB))
    part = call(
        functools.partial(first_body, hubs, 256), shape((slab, width), F32), got, hub_mat, sparse_mat,
        flops=products * width * 2,
    )
    got = exchange(call(pick_sum_body, packet, part, swap(part), hub_row, slot_row))
    hid_hub, hid_slot = call(
        functools.partial(hidden_body, hubs), (shape((hub_cols, hid), BF16), shape((slot_cols, hid), BF16)), got, w_in
    )

    def aggregate(away):
        return call(
            functools.partial(second_body, 256, away), shape((half, hid), F32), hid_hub, hid_slot, hub_mat, sparse_mat,
            flops=products * hid // 2,
        )

    away = swap(aggregate(True))
    part = aggregate(False)
    scale = float(1.0 / (slab * nrows) ** 0.5)
    logits, dsec, grad_out = call(
        functools.partial(score_body, scale),
        (shape((classes, half), BF16), shape((hid, half), BF16), shape((classes, hid), F32)),
        part, away, w_out.T, labels.reshape(1, half),
    )
    oth = swap(dsec)
    grad_in = call(
        functools.partial(back_body, hubs, 512), shape((width, hid), F32),
        dsec, oth, got, w_in, hub_mat, sparse_mat,
        scratch=[pltpu.VMEM((hid, slab), BF16), pltpu.VMEM((hid, width), F32)], flops=products * hid,
    )
    flat = jnp.concatenate([grad_in, grad_out], axis=0)
    count = width + classes
    share = -(-count // nrows)
    flat = jnp.pad(flat, ((0, share * nrows - count), (0, 0))).reshape(nrows, share, hid)
    mine = exchange(flat).sum(axis=0)
    mine = mine + swap(mine)
    whole = exchange(jnp.broadcast_to(mine[None], (nrows, share, hid))).reshape(nrows * share, hid)
    return (logits.T, whole[:width], whole[width:count].T)


def solution(mesh):
    return jax.shard_map(
        on_device,
        mesh=mesh,
        in_specs=(
            P("rows", None),
            P(),
            P(),
            P(("rows", "rep")),
            P("rows", "rep", None),
            P("rows", "rep", None),
            P("rows", "rep", None),
            P("rows", "rep", None),
        ),
        out_specs=(P(("rows", "rep"), None), P(), P()),
        check_vma=False,
    )
```

```python
import functools
import jax
import jax.numpy as jnp
from jax import lax
from jax.experimental import pallas as pl
from jax.experimental.pallas import tpu as pltpu
from jax.sharding import PartitionSpec as P

SWAP = [(0, 1), (1, 0)]
F32, BF16 = jnp.float32, jnp.bfloat16
VM = pl.BlockSpec(memory_space=pltpu.VMEM)
MIB = 1024 * 1024
STEP1 = 2048
STEP2 = 1024
STEP3 = 2048


def dot(a, b):
    return jnp.dot(a, b, preferred_element_type=F32)


def dot_t(a, b):
    return lax.dot_general(a, b, (((1,), (1,)), ((), ())), preferred_element_type=F32)


def call(body, outs, *args, flops=0, traffic=0, scratch=(), limit=16):
    return pl.pallas_call(
        body,
        out_shape=outs,
        in_specs=[VM] * len(args),
        out_specs=jax.tree.map(lambda _: VM, outs),
        scratch_shapes=scratch,
        compiler_params=pltpu.CompilerParams(vmem_limit_bytes=limit * MIB),
        cost_estimate=pl.CostEstimate(flops=flops, bytes_accessed=traffic, transcendentals=0),
    )(*args)


def one_hot(row, slab):
    count = row.shape[1]
    index = jnp.broadcast_to(row, (128, count)).T
    wide = jnp.concatenate([index] * (slab // 128), axis=1)
    return (wide == lax.broadcasted_iota(jnp.int32, (count, slab), 1)).astype(BF16)


def spread(values, hub_ref, slot_ref, out_ref):
    peers, rows, width = out_ref.shape
    hubs = hub_ref.shape[1]
    slab = values.shape[0]
    hub = dot(one_hot(hub_ref[...], slab), values)
    slot = dot(one_hot(slot_ref[...], slab), values)
    whole = jnp.concatenate(
        [
            jnp.broadcast_to(hub[None], (peers, hubs, width)),
            slot.reshape(peers, rows - hubs, width),
        ],
        axis=1,
    )
    out_ref[...] = whole.astype(BF16)


def pick_body(feat_hbm, hub_hbm, slot_hbm, out_ref, feat_ref, hub_ref, slot_ref, sems):
    pairs = ((hub_hbm, hub_ref), (slot_hbm, slot_ref), (feat_hbm, feat_ref))
    copies = [pltpu.make_async_copy(src, dst, sems.at[i]) for i, (src, dst) in enumerate(pairs)]
    for copy in copies:
        copy.start()
    for copy in copies:
        copy.wait()
    spread(feat_ref[...], hub_ref, slot_ref, out_ref)


def pick(packet, feats, hub_row, slot_row, flops):
    return pl.pallas_call(
        pick_body,
        out_shape=packet,
        in_specs=[pl.BlockSpec(memory_space=pl.ANY)] * 3,
        out_specs=VM,
        scratch_shapes=[pltpu.VMEM(x.shape, x.dtype) for x in (feats, hub_row, slot_row)]
        + [pltpu.SemaphoreType.DMA((3,))],
        compiler_params=pltpu.CompilerParams(vmem_limit_bytes=16 * MIB),
        cost_estimate=pl.CostEstimate(flops=flops, bytes_accessed=0, transcendentals=0),
    )(*(pltpu.with_memory_space_constraint(x, pltpu.HBM) for x in (feats, hub_row, slot_row)))


def pick_sum_body(part_ref, away_ref, hub_ref, slot_ref, out_ref):
    spread((part_ref[...] + away_ref[...]).astype(BF16), hub_ref, slot_ref, out_ref)


def split(got_ref, hubs):
    peers, rows, width = got_ref.shape
    hub = got_ref[:, :hubs, :].reshape(peers * hubs, width)
    slot = got_ref[:, hubs:, :].astype(F32).reshape(peers * (rows - hubs), width).astype(BF16)
    return hub, slot


def first_body(hubs, step, got_ref, hub_mat, sparse_mat, part_ref):
    hub, slot = split(got_ref, hubs)

    @pl.loop(0, part_ref.shape[0] // step)
    def _(i):
        at = pl.ds(pl.multiple_of(i * step, step), step)
        part_ref[at, :] = dot(hub_mat[at, :], hub) + dot(sparse_mat[at, :], slot)


def second_rows(step, start, part_ref, hid_hub, hid_slot, hub_mat, sparse_mat):
    @pl.loop(0, part_ref.shape[0] // step)
    def _(i):
        at = pl.ds(pl.multiple_of(i * step, step), step)
        src = pl.ds(pl.multiple_of(start + i * step, step), step)
        part_ref[at, :] = dot(hub_mat[src, :], hid_hub[...]) + dot(sparse_mat[src, :], hid_slot[...])


def away_body(hubs, step, got_ref, w_ref, hub_mat, sparse_mat, part_ref, hid_hub, hid_slot):
    hub, slot = split(got_ref, hubs)
    hid_hub[...] = jnp.maximum(dot(hub, w_ref[...]), 0.0).astype(BF16)
    hid_slot[...] = jnp.maximum(dot(slot, w_ref[...]), 0.0).astype(BF16)
    start = (1 - lax.axis_index("rep")) * part_ref.shape[0]
    second_rows(step, start, part_ref, hid_hub, hid_slot, hub_mat, sparse_mat)


def own_body(step, hid_hub, hid_slot, hub_mat, sparse_mat, part_ref):
    start = lax.axis_index("rep") * part_ref.shape[0]
    second_rows(step, start, part_ref, hid_hub, hid_slot, hub_mat, sparse_mat)


def score_body(scale, part_ref, away_ref, w_ref, label_ref, logit_ref, dsec_ref, grad_ref):
    second = (part_ref[...] + away_ref[...]).astype(BF16)
    scores = dot_t(w_ref[...], second)
    logit_ref[...] = scores.astype(BF16)
    top = jnp.max(scores, axis=0, keepdims=True)
    expo = jnp.exp(scores - top)
    probs = expo / jnp.sum(expo, axis=0, keepdims=True)
    hot = label_ref[...] == lax.broadcasted_iota(jnp.int32, scores.shape, 0)
    dscore = (probs - hot.astype(F32)) * scale
    high = dscore.astype(BF16)
    low = (dscore - high.astype(F32)).astype(BF16)
    grad_ref[...] = dot(high, second) + dot(low, second)
    dsec_ref[...] = lax.dot_general(
        w_ref[...], high, (((0,), (0,)), ((), ())), preferred_element_type=F32
    ).astype(BF16)


def back_rows(hubs, step, start, dsec_ref, got_ref, w_ref, hub_mat, sparse_mat, acc_ref):
    half = dsec_ref.shape[1]
    peers, rows, width = got_ref.shape
    w_t = w_ref[...].astype(F32).T.astype(BF16)
    src = pl.ds(pl.multiple_of(start, half), half)

    def term(cols, mat):
        hid = dot_t(w_t, cols)
        grad = jnp.where(hid > 0, dot(dsec_ref[...], mat), 0.0).astype(BF16)
        return dot(grad, cols)

    slot = got_ref[:, hubs:, :].astype(F32).reshape(peers * (rows - hubs), width).astype(BF16)
    acc_ref[...] = term(slot, sparse_mat[src, :])
    group = step // hubs

    @pl.loop(0, hub_mat.shape[1] // step)
    def _(i):
        at = pl.ds(pl.multiple_of(i * step, step), step)
        cols = got_ref[pl.ds(i * group, group), :hubs, :].reshape(step, width)
        acc_ref[...] += term(cols, hub_mat[src, at])


def back_own_body(hubs, step, dsec_ref, got_ref, w_ref, hub_mat, sparse_mat, acc_ref):
    start = lax.axis_index("rep") * dsec_ref.shape[1]
    back_rows(hubs, step, start, dsec_ref, got_ref, w_ref, hub_mat, sparse_mat, acc_ref)


def back_away_body(hubs, step, own_ref, grad_ref, dsec_ref, got_ref, w_ref, hub_mat, sparse_mat, out_ref, acc_ref):
    start = (1 - lax.axis_index("rep")) * dsec_ref.shape[1]
    back_rows(hubs, step, start, dsec_ref, got_ref, w_ref, hub_mat, sparse_mat, acc_ref)
    width = got_ref.shape[2]
    classes = grad_ref.shape[0]
    out_ref[:width, :] = (acc_ref[...] + own_ref[...]).T
    out_ref[width : width + classes, :] = grad_ref[...]
    rest = out_ref.shape[0] - width - classes
    out_ref[width + classes :, :] = jnp.zeros((rest, out_ref.shape[1]), F32)


def sum_body(got_ref, out_ref):
    out_ref[...] = jnp.sum(got_ref[...], axis=0)


def share_body(mine_ref, away_ref, out_ref):
    out_ref[...] = jnp.broadcast_to((mine_ref[...] + away_ref[...])[None], out_ref.shape)


def on_device(node_feats, w_in, w_out, labels, hub_rows, send_rows, adj_hub, adj_sparse):
    nrows = lax.axis_size("rows")
    slab, width = node_feats.shape
    half = slab // lax.axis_size("rep")
    hid, classes = w_out.shape
    hubs = hub_rows.shape[2]
    slots = send_rows.shape[2] // nrows
    hub_cols, slot_cols = nrows * hubs, nrows * slots
    hub_row = hub_rows.reshape(1, hubs)
    slot_row = send_rows.reshape(1, slot_cols)
    hub_mat = pltpu.with_memory_space_constraint(adj_hub.reshape(slab, hub_cols), pltpu.VMEM)
    sparse_mat = pltpu.with_memory_space_constraint(adj_sparse.reshape(slab, slot_cols), pltpu.VMEM)
    shape = jax.ShapeDtypeStruct
    packet = shape((nrows, hubs + slots, width), BF16)
    products = 2 * slab * (hub_cols + slot_cols)

    def exchange(x):
        return lax.all_to_all(x, "rows", split_axis=0, concat_axis=0, tiled=True)

    def swap(x):
        return lax.ppermute(x, "rep", SWAP)

    got = exchange(pick(packet, node_feats, hub_row, slot_row, products * 256))
    part = call(
        functools.partial(first_body, hubs, STEP1), shape((slab, width), F32), got, hub_mat, sparse_mat,
        flops=products * width * 2,
    )
    got = exchange(call(pick_sum_body, packet, part, swap(part), hub_row, slot_row))
    part, hid_hub, hid_slot = call(
        functools.partial(away_body, hubs, STEP2),
        (shape((half, hid), F32), shape((hub_cols, hid), BF16), shape((slot_cols, hid), BF16)),
        got, w_in, hub_mat, sparse_mat,
        flops=products * hid // 2,
    )
    away = swap(part)
    part = call(
        functools.partial(own_body, STEP2), shape((half, hid), F32), hid_hub, hid_slot, hub_mat, sparse_mat,
        flops=products * hid // 2,
    )
    scale = float(1.0 / (slab * nrows) ** 0.5)
    logits, dsec, grad_out = call(
        functools.partial(score_body, scale),
        (shape((classes, half), BF16), shape((hid, half), BF16), shape((classes, hid), F32)),
        part, away, w_out.T, labels.reshape(1, half),
    )
    oth = swap(dsec)
    own = call(
        functools.partial(back_own_body, hubs, STEP3), shape((hid, width), F32), dsec, got, w_in, hub_mat, sparse_mat,
        flops=products * hid // 2,
    )
    count = width + classes
    share = -(-count // (8 * nrows)) * 8
    flat = call(
        functools.partial(back_away_body, hubs, STEP3), shape((share * nrows, hid), F32),
        own, grad_out, oth, got, w_in, hub_mat, sparse_mat,
        scratch=[pltpu.VMEM((hid, width), F32)], flops=products * hid // 2,
    )
    mine = call(sum_body, shape((share, hid), F32), exchange(flat.reshape(nrows, share, hid)))
    whole = call(share_body, shape((nrows, share, hid), F32), mine, swap(mine))
    whole = exchange(whole).reshape(nrows * share, hid)
    return (logits.T, whole[:width], whole[width:count].T)


def solution(mesh):
    return jax.shard_map(
        on_device,
        mesh=mesh,
        in_specs=(
            P("rows", None),
            P(),
            P(),
            P(("rows", "rep")),
            P("rows", "rep", None),
            P("rows", "rep", None),
            P("rows", "rep", None),
            P("rows", "rep", None),
        ),
        out_specs=(P(("rows", "rep"), None), P(), P()),
        check_vma=False,
    )
```

```python
import functools
import jax
import jax.numpy as jnp
from jax import lax
from jax.experimental import pallas as pl
from jax.experimental.pallas import tpu as pltpu
from jax.sharding import PartitionSpec as P

SWAP = [(0, 1), (1, 0)]
F32, BF16 = jnp.float32, jnp.bfloat16
VM = pl.BlockSpec(memory_space=pltpu.VMEM)
MIB = 1024 * 1024
STEP1 = 2048
STEP2 = 1024
STEP3 = 2048


def dot(a, b):
    return jnp.dot(a, b, preferred_element_type=F32)


def dot_t(a, b):
    return lax.dot_general(a, b, (((1,), (1,)), ((), ())), preferred_element_type=F32)


def call(body, outs, *args, flops=0, traffic=0, scratch=(), limit=16):
    return pl.pallas_call(
        body,
        out_shape=outs,
        in_specs=[VM] * len(args),
        out_specs=jax.tree.map(lambda _: VM, outs),
        scratch_shapes=scratch,
        compiler_params=pltpu.CompilerParams(vmem_limit_bytes=limit * MIB),
        cost_estimate=pl.CostEstimate(flops=flops, bytes_accessed=traffic, transcendentals=0),
    )(*args)


def one_hot(row, slab):
    count = row.shape[1]
    index = jnp.broadcast_to(row, (128, count)).T
    wide = jnp.concatenate([index] * (slab // 128), axis=1)
    return (wide == lax.broadcasted_iota(jnp.int32, (count, slab), 1)).astype(BF16)


def spread(hub, slot, out_ref):
    peers, rows, width = out_ref.shape
    hubs = hub.shape[0]
    whole = jnp.concatenate(
        [
            jnp.broadcast_to(hub[None], (peers, hubs, width)),
            slot.reshape(peers, rows - hubs, width),
        ],
        axis=1,
    )
    out_ref[...] = whole.astype(BF16)


def pick_body(feat_hbm, hub_hbm, slot_hbm, out_ref, feat_ref, hub_ref, slot_ref, sems):
    pairs = ((hub_hbm, hub_ref), (slot_hbm, slot_ref), (feat_hbm, feat_ref))
    copies = [pltpu.make_async_copy(src, dst, sems.at[i]) for i, (src, dst) in enumerate(pairs)]
    for copy in copies:
        copy.start()
    copies[0].wait()
    copies[1].wait()
    slab = feat_ref.shape[0]
    hub_hot = one_hot(hub_ref[...], slab)
    slot_hot = one_hot(slot_ref[...], slab)
    copies[2].wait()
    spread(dot(hub_hot, feat_ref[...]), dot(slot_hot, feat_ref[...]), out_ref)


def pick_sum_body(part_ref, away_ref, hub_ref, slot_ref, out_ref):
    values = (part_ref[...] + away_ref[...]).astype(BF16)
    slab = values.shape[0]
    spread(dot(one_hot(hub_ref[...], slab), values), dot(one_hot(slot_ref[...], slab), values), out_ref)


def pick(packet, feats, hub_row, slot_row, flops):
    return pl.pallas_call(
        pick_body,
        out_shape=packet,
        in_specs=[pl.BlockSpec(memory_space=pl.ANY)] * 3,
        out_specs=VM,
        scratch_shapes=[pltpu.VMEM(x.shape, x.dtype) for x in (feats, hub_row, slot_row)]
        + [pltpu.SemaphoreType.DMA((3,))],
        compiler_params=pltpu.CompilerParams(vmem_limit_bytes=16 * MIB),
        cost_estimate=pl.CostEstimate(flops=flops, bytes_accessed=0, transcendentals=0),
    )(*(pltpu.with_memory_space_constraint(x, pltpu.HBM) for x in (feats, hub_row, slot_row)))


def split(got_ref, hubs):
    peers, rows, width = got_ref.shape
    hub = got_ref[:, :hubs, :].reshape(peers * hubs, width)
    slot = got_ref[:, hubs:, :].astype(F32).reshape(peers * (rows - hubs), width).astype(BF16)
    return hub, slot


def first_body(hubs, step, got_ref, hub_mat, sparse_mat, part_ref):
    hub, slot = split(got_ref, hubs)

    @pl.loop(0, part_ref.shape[0] // step)
    def _(i):
        at = pl.ds(pl.multiple_of(i * step, step), step)
        part_ref[at, :] = dot(hub_mat[at, :], hub) + dot(sparse_mat[at, :], slot)


def second_rows(step, start, part_ref, hid_hub, hid_slot, hub_mat, sparse_mat):
    @pl.loop(0, part_ref.shape[0] // step)
    def _(i):
        at = pl.ds(pl.multiple_of(i * step, step), step)
        src = pl.ds(pl.multiple_of(start + i * step, step), step)
        part_ref[at, :] = dot(hub_mat[src, :], hid_hub[...]) + dot(sparse_mat[src, :], hid_slot[...])


def away_body(hubs, step, got_ref, w_ref, hub_mat, sparse_mat, part_ref, hid_hub, hid_slot):
    hub, slot = split(got_ref, hubs)
    hid_hub[...] = jnp.maximum(dot(hub, w_ref[...]), 0.0).astype(BF16)
    hid_slot[...] = jnp.maximum(dot(slot, w_ref[...]), 0.0).astype(BF16)
    start = (1 - lax.axis_index("rep")) * part_ref.shape[0]
    second_rows(step, start, part_ref, hid_hub, hid_slot, hub_mat, sparse_mat)


def own_body(step, hid_hub, hid_slot, hub_mat, sparse_mat, part_ref):
    start = lax.axis_index("rep") * part_ref.shape[0]
    second_rows(step, start, part_ref, hid_hub, hid_slot, hub_mat, sparse_mat)


def score_body(scale, part_ref, away_ref, w_ref, label_ref, logit_ref, dsec_ref, grad_ref):
    second = (part_ref[...] + away_ref[...]).astype(BF16)
    scores = dot_t(w_ref[...], second)
    logit_ref[...] = scores.astype(BF16)
    top = jnp.max(scores, axis=0, keepdims=True)
    expo = jnp.exp(scores - top)
    probs = expo / jnp.sum(expo, axis=0, keepdims=True)
    hot = label_ref[...] == lax.broadcasted_iota(jnp.int32, scores.shape, 0)
    dscore = (probs - hot.astype(F32)) * scale
    high = dscore.astype(BF16)
    low = (dscore - high.astype(F32)).astype(BF16)
    grad_ref[...] = dot(high, second) + dot(low, second)
    dsec_ref[...] = lax.dot_general(
        w_ref[...], high, (((0,), (0,)), ((), ())), preferred_element_type=F32
    ).astype(BF16)


def back_own_body(step, dsec_ref, hub_mat, sparse_mat, hub_out, slot_out):
    half = dsec_ref.shape[1]
    src = pl.ds(pl.multiple_of(lax.axis_index("rep") * half, half), half)
    slot_out[...] = dot(dsec_ref[...], sparse_mat[src, :])

    @pl.loop(0, hub_mat.shape[1] // step)
    def _(i):
        at = pl.ds(pl.multiple_of(i * step, step), step)
        hub_out[:, at] = dot(dsec_ref[...], hub_mat[src, at])


def back_away_body(
    hubs, step, hub_own, slot_own, grad_ref, dsec_ref, got_ref, w_ref, hub_mat, sparse_mat, out_ref, acc_ref
):
    half = dsec_ref.shape[1]
    src = pl.ds(pl.multiple_of((1 - lax.axis_index("rep")) * half, half), half)
    peers, rows, width = got_ref.shape
    w_t = w_ref[...].astype(F32).T.astype(BF16)

    def term(cols, mat, own):
        hid = dot_t(w_t, cols)
        grad = jnp.where(hid > 0, dot(dsec_ref[...], mat) + own, 0.0).astype(BF16)
        return dot(grad, cols)

    slot = got_ref[:, hubs:, :].astype(F32).reshape(peers * (rows - hubs), width).astype(BF16)
    acc_ref[...] = term(slot, sparse_mat[src, :], slot_own[...])
    group = step // hubs

    @pl.loop(0, hub_mat.shape[1] // step)
    def _(i):
        at = pl.ds(pl.multiple_of(i * step, step), step)
        cols = got_ref[pl.ds(i * group, group), :hubs, :].reshape(step, width)
        acc_ref[...] += term(cols, hub_mat[src, at], hub_own[:, at])

    classes = grad_ref.shape[0]
    out_ref[:width, :] = acc_ref[...].T
    out_ref[width : width + classes, :] = grad_ref[...]
    rest = out_ref.shape[0] - width - classes
    out_ref[width + classes :, :] = jnp.zeros((rest, out_ref.shape[1]), F32)


def sum_body(got_ref, out_ref):
    out_ref[...] = jnp.sum(got_ref[...], axis=0)


def share_body(mine_ref, away_ref, out_ref):
    mine = (mine_ref[...] + away_ref[...]).astype(BF16).astype(F32)
    out_ref[...] = jnp.broadcast_to(mine[None], out_ref.shape).astype(BF16)


def parts_body(got_ref, in_ref, out_ref):
    peers, rows, width = got_ref.shape
    whole = got_ref[...].astype(F32).reshape(peers * rows, width)
    first, second = in_ref.shape[0], out_ref.shape[0]
    in_ref[...] = whole[:first]
    out_ref[...] = whole[first : first + second]


def on_device(node_feats, w_in, w_out, labels, hub_rows, send_rows, adj_hub, adj_sparse):
    nrows = lax.axis_size("rows")
    slab, width = node_feats.shape
    half = slab // lax.axis_size("rep")
    hid, classes = w_out.shape
    hubs = hub_rows.shape[2]
    slots = send_rows.shape[2] // nrows
    hub_cols, slot_cols = nrows * hubs, nrows * slots
    hub_row = hub_rows.reshape(1, hubs)
    slot_row = send_rows.reshape(1, slot_cols)
    hub_mat = pltpu.with_memory_space_constraint(adj_hub.reshape(slab, hub_cols), pltpu.VMEM)
    sparse_mat = pltpu.with_memory_space_constraint(adj_sparse.reshape(slab, slot_cols), pltpu.VMEM)
    shape = jax.ShapeDtypeStruct
    packet = shape((nrows, hubs + slots, width), BF16)
    products = 2 * slab * (hub_cols + slot_cols)

    def exchange(x):
        return lax.all_to_all(x, "rows", split_axis=0, concat_axis=0, tiled=True)

    def swap(x):
        return lax.ppermute(x, "rep", SWAP)

    got = exchange(pick(packet, node_feats, hub_row, slot_row, products * 256))
    part = call(
        functools.partial(first_body, hubs, STEP1), shape((slab, width), F32), got, hub_mat, sparse_mat,
        flops=products * width * 2,
    )
    got = exchange(call(pick_sum_body, packet, part, swap(part), hub_row, slot_row))
    part, hid_hub, hid_slot = call(
        functools.partial(away_body, hubs, STEP2),
        (shape((half, hid), F32), shape((hub_cols, hid), BF16), shape((slot_cols, hid), BF16)),
        got, w_in, hub_mat, sparse_mat,
        flops=products * hid // 2,
    )
    away = swap(part)
    part = call(
        functools.partial(own_body, STEP2), shape((half, hid), F32), hid_hub, hid_slot, hub_mat, sparse_mat,
        flops=products * hid // 2,
    )
    scale = float(1.0 / (slab * nrows) ** 0.5)
    logits, dsec, grad_out = call(
        functools.partial(score_body, scale),
        (shape((classes, half), BF16), shape((hid, half), BF16), shape((classes, hid), F32)),
        part, away, w_out.T, labels.reshape(1, half),
    )
    oth = swap(dsec)
    hub_own, slot_own = call(
        functools.partial(back_own_body, STEP3), (shape((hid, hub_cols), F32), shape((hid, slot_cols), F32)),
        dsec, hub_mat, sparse_mat,
        flops=products * hid // 2,
    )
    count = width + classes
    share = -(-count // (8 * nrows)) * 8
    flat = call(
        functools.partial(back_away_body, hubs, STEP3), shape((share * nrows, hid), F32),
        hub_own, slot_own, grad_out, oth, got, w_in, hub_mat, sparse_mat,
        scratch=[pltpu.VMEM((hid, width), F32)], flops=products * hid // 2,
    )
    mine = call(sum_body, shape((share, hid), F32), exchange(flat.reshape(nrows, share, hid)))
    whole = exchange(call(share_body, shape((nrows, share, hid), BF16), mine, swap(mine)))
    grad_in, grad_out = call(parts_body, (shape((width, hid), F32), shape((classes, hid), F32)), whole)
    return (logits.T, grad_in, grad_out.T)


def solution(mesh):
    return jax.shard_map(
        on_device,
        mesh=mesh,
        in_specs=(
            P("rows", None),
            P(),
            P(),
            P(("rows", "rep")),
            P("rows", "rep", None),
            P("rows", "rep", None),
            P("rows", "rep", None),
            P("rows", "rep", None),
        ),
        out_specs=(P(("rows", "rep"), None), P(), P()),
        check_vma=False,
    )
```

```python
import functools
import jax
import jax.numpy as jnp
from jax import lax
from jax.experimental import pallas as pl
from jax.experimental.pallas import tpu as pltpu
from jax.sharding import PartitionSpec as P

SWAP = [(0, 1), (1, 0)]
F32, BF16 = jnp.float32, jnp.bfloat16
VM = pl.BlockSpec(memory_space=pltpu.VMEM)
MIB = 1024 * 1024
PIECES = 1
TOP = 6
STEP1 = 1024
STEP2 = 512
STEP3 = 4096
STEP4 = 4096


def dot(a, b):
    return jnp.dot(a, b, preferred_element_type=F32)


def dot_t(a, b):
    return lax.dot_general(a, b, (((1,), (1,)), ((), ())), preferred_element_type=F32)


def call(body, outs, *args, flops=0, traffic=0, scratch=(), limit=16):
    return pl.pallas_call(
        body,
        out_shape=outs,
        in_specs=[VM] * len(args),
        out_specs=jax.tree.map(lambda _: VM, outs),
        scratch_shapes=scratch,
        compiler_params=pltpu.CompilerParams(vmem_limit_bytes=limit * MIB),
        cost_estimate=pl.CostEstimate(flops=flops, bytes_accessed=traffic, transcendentals=0),
    )(*args)


def one_hot(row, slab):
    count = row.shape[1]
    index = jnp.broadcast_to(row, (128, count)).T
    wide = jnp.concatenate([index] * (slab // 128), axis=1)
    return (wide == lax.broadcasted_iota(jnp.int32, (count, slab), 1)).astype(BF16)


def spread(hub, slot, out_ref):
    peers, rows, width = out_ref.shape
    hubs = hub.shape[0]
    whole = jnp.concatenate(
        [
            jnp.broadcast_to(hub[None], (peers, hubs, width)),
            slot.reshape(peers, rows - hubs, width),
        ],
        axis=1,
    )
    out_ref[...] = whole.astype(BF16)


def pick_body(feat_hbm, hub_hbm, slot_hbm, out_ref, hub_hot, slot_hot, feat_ref, hub_ref, slot_ref, sems):
    slab = feat_ref.shape[0]
    rows = slab // PIECES
    copies = [
        pltpu.make_async_copy(hub_hbm, hub_ref, sems.at[PIECES]),
        pltpu.make_async_copy(slot_hbm, slot_ref, sems.at[PIECES + 1]),
    ]
    for i in range(PIECES):
        at = pl.ds(i * rows, rows)
        copies.append(pltpu.make_async_copy(feat_hbm.at[at], feat_ref.at[at], sems.at[i]))
    for copy in copies:
        copy.start()
    copies[0].wait()
    copies[1].wait()
    hub_hot[...] = one_hot(hub_ref[...], slab)
    slot_hot[...] = one_hot(slot_ref[...], slab)
    hub = slot = 0.0
    for i in range(PIECES):
        at = pl.ds(i * rows, rows)
        copies[2 + i].wait()
        hub += dot(hub_hot[:, at], feat_ref[at, :])
        slot += dot(slot_hot[:, at], feat_ref[at, :])
    spread(hub, slot, out_ref)


def pick(packet, feats, hub_row, slot_row, flops):
    return pl.pallas_call(
        pick_body,
        out_shape=(packet,)
        + tuple(jax.ShapeDtypeStruct((x.shape[1], feats.shape[0]), BF16) for x in (hub_row, slot_row)),
        in_specs=[pl.BlockSpec(memory_space=pl.ANY)] * 3,
        out_specs=(VM, VM, VM),
        scratch_shapes=[pltpu.VMEM(x.shape, x.dtype) for x in (feats, hub_row, slot_row)]
        + [pltpu.SemaphoreType.DMA((PIECES + 2,))],
        compiler_params=pltpu.CompilerParams(vmem_limit_bytes=16 * MIB),
        cost_estimate=pl.CostEstimate(flops=flops, bytes_accessed=0, transcendentals=0),
    )(*(pltpu.with_memory_space_constraint(x, pltpu.HBM) for x in (feats, hub_row, slot_row)))


def pick_top_body(part_ref, away_ref, hub_hot, slot_hot, hub_ref, slot_ref):
    values = (part_ref[...] + away_ref[...]).astype(BF16)
    top = pl.ds(0, values.shape[0])
    hub_ref[...] = dot(hub_hot[:, top], values)
    slot_ref[...] = dot(slot_hot[:, top], values)


def pick_rest_body(part_ref, away_ref, hub_hot, slot_hot, hub_ref, slot_ref, out_ref):
    values = (part_ref[...] + away_ref[...]).astype(BF16)
    count = values.shape[0]
    rest = pl.ds(hub_hot.shape[1] - count, count)
    hub = hub_ref[...] + dot(hub_hot[:, rest], values)
    slot = slot_ref[...] + dot(slot_hot[:, rest], values)
    spread(hub, slot, out_ref)


def split(got_ref, hubs):
    peers, rows, width = got_ref.shape
    hub = got_ref[:, :hubs, :].reshape(peers * hubs, width)
    slot = got_ref[:, hubs:, :].astype(F32).reshape(peers * (rows - hubs), width).astype(BF16)
    return hub, slot


def first_body(hubs, start, got_ref, hub_mat, sparse_mat, part_ref):
    hub, slot = split(got_ref, hubs)
    at = pl.ds(start, part_ref.shape[0])
    part_ref[...] = dot(hub_mat[at, :], hub) + dot(sparse_mat[at, :], slot)


def second_rows(step, start, part_ref, hid_hub, hid_slot, hub_mat, sparse_mat):
    @pl.loop(0, part_ref.shape[0] // step)
    def _(i):
        at = pl.ds(pl.multiple_of(i * step, step), step)
        src = pl.ds(pl.multiple_of(start + i * step, step), step)
        part_ref[at, :] = dot(hub_mat[src, :], hid_hub[...]) + dot(sparse_mat[src, :], hid_slot[...])


def away_body(hubs, step, got_ref, w_ref, hub_mat, sparse_mat, part_ref, hid_hub, hid_slot):
    hub, slot = split(got_ref, hubs)
    hid_hub[...] = jnp.maximum(dot(hub, w_ref[...]), 0.0).astype(BF16)
    hid_slot[...] = jnp.maximum(dot(slot, w_ref[...]), 0.0).astype(BF16)
    start = (1 - lax.axis_index("rep")) * part_ref.shape[0]
    second_rows(step, start, part_ref, hid_hub, hid_slot, hub_mat, sparse_mat)


def own_body(step, hid_hub, hid_slot, hub_mat, sparse_mat, part_ref):
    start = lax.axis_index("rep") * part_ref.shape[0]
    second_rows(step, start, part_ref, hid_hub, hid_slot, hub_mat, sparse_mat)


def score_body(scale, part_ref, away_ref, w_ref, label_ref, logit_ref, dsec_ref, grad_ref):
    second = (part_ref[...] + away_ref[...]).astype(BF16)
    scores = dot_t(w_ref[...], second)
    logit_ref[...] = scores.astype(BF16)
    top = jnp.max(scores, axis=0, keepdims=True)
    expo = jnp.exp(scores - top)
    probs = expo / jnp.sum(expo, axis=0, keepdims=True)
    hot = label_ref[...] == lax.broadcasted_iota(jnp.int32, scores.shape, 0)
    dscore = (probs - hot.astype(F32)) * scale
    high = dscore.astype(BF16)
    low = (dscore - high.astype(F32)).astype(BF16)
    grad_ref[...] = dot(high, second) + dot(low, second)
    dsec_ref[...] = lax.dot_general(
        w_ref[...], high, (((0,), (0,)), ((), ())), preferred_element_type=F32
    ).astype(BF16)


def back_own_body(step, dsec_ref, hub_mat, sparse_mat, hub_out, slot_out):
    half = dsec_ref.shape[1]
    src = pl.ds(pl.multiple_of(lax.axis_index("rep") * half, half), half)
    slot_out[...] = dot(dsec_ref[...], sparse_mat[src, :])

    @pl.loop(0, hub_mat.shape[1] // step)
    def _(i):
        at = pl.ds(pl.multiple_of(i * step, step), step)
        hub_out[:, at] = dot(dsec_ref[...], hub_mat[src, at])


def back_away_body(
    hubs, step, hub_own, slot_own, grad_ref, dsec_ref, got_ref, w_ref, hub_mat, sparse_mat, out_ref, acc_ref
):
    half = dsec_ref.shape[1]
    src = pl.ds(pl.multiple_of((1 - lax.axis_index("rep")) * half, half), half)
    peers, rows, width = got_ref.shape
    w_t = w_ref[...].astype(F32).T.astype(BF16)

    def term(cols, mat, own):
        hid = dot_t(w_t, cols)
        grad = jnp.where(hid > 0, dot(dsec_ref[...], mat) + own, 0.0).astype(BF16)
        return dot(grad, cols)

    slot = got_ref[:, hubs:, :].astype(F32).reshape(peers * (rows - hubs), width).astype(BF16)
    acc_ref[...] = term(slot, sparse_mat[src, :], slot_own[...])
    group = step // hubs

    @pl.loop(0, hub_mat.shape[1] // step)
    def _(i):
        at = pl.ds(pl.multiple_of(i * step, step), step)
        cols = got_ref[pl.ds(i * group, group), :hubs, :].reshape(step, width)
        acc_ref[...] += term(cols, hub_mat[src, at], hub_own[:, at])

    classes = grad_ref.shape[0]
    rest = out_ref.shape[0] * out_ref.shape[1] - width - classes
    flat = jnp.concatenate([acc_ref[...].T, grad_ref[...], jnp.zeros((rest, out_ref.shape[2]), F32)], axis=0)
    out_ref[...] = flat.reshape(out_ref.shape).astype(BF16)


def sum_body(got_ref, out_ref):
    out_ref[...] = jnp.sum(got_ref[...].astype(F32), axis=0)


def share_body(mine_ref, away_ref, out_ref):
    mine = (mine_ref[...] + away_ref[...]).astype(BF16).astype(F32)
    out_ref[...] = jnp.broadcast_to(mine[None], out_ref.shape).astype(BF16)


def parts_body(got_ref, in_ref, out_ref):
    peers, rows, width = got_ref.shape
    whole = got_ref[...].astype(F32).reshape(peers * rows, width)
    first, second = in_ref.shape[0], out_ref.shape[0]
    in_ref[...] = whole[:first]
    out_ref[...] = whole[first : first + second]


def on_device(node_feats, w_in, w_out, labels, hub_rows, send_rows, adj_hub, adj_sparse):
    nrows = lax.axis_size("rows")
    slab, width = node_feats.shape
    half = slab // lax.axis_size("rep")
    hid, classes = w_out.shape
    hubs = hub_rows.shape[2]
    slots = send_rows.shape[2] // nrows
    hub_cols, slot_cols = nrows * hubs, nrows * slots
    hub_row = hub_rows.reshape(1, hubs)
    slot_row = send_rows.reshape(1, slot_cols)
    hub_mat = pltpu.with_memory_space_constraint(adj_hub.reshape(slab, hub_cols), pltpu.VMEM)
    sparse_mat = pltpu.with_memory_space_constraint(adj_sparse.reshape(slab, slot_cols), pltpu.VMEM)
    shape = jax.ShapeDtypeStruct
    packet = shape((nrows, hubs + slots, width), BF16)
    products = 2 * slab * (hub_cols + slot_cols)

    def exchange(x):
        return lax.all_to_all(x, "rows", split_axis=0, concat_axis=0, tiled=True)

    def swap(x):
        return lax.ppermute(x, "rep", SWAP)

    sent, hub_hot, slot_hot = pick(packet, node_feats, hub_row, slot_row, products * 256)
    got = exchange(sent)

    def first_rows(start, rows):
        return call(
            functools.partial(first_body, hubs, start), shape((rows, width), F32), got, hub_mat, sparse_mat,
            flops=products * rows // slab * width * 2,
        )

    top = slab * TOP // 8
    part = first_rows(0, top)
    away = swap(part)
    part_rest = first_rows(top, slab - top)
    away_rest = swap(part_rest)
    hub_some, slot_some = call(
        pick_top_body, (shape((hubs, width), F32), shape((slot_cols, width), F32)), part, away, hub_hot, slot_hot,
        flops=2 * (hubs + slot_cols) * slab * width,
    )
    got = exchange(call(pick_rest_body, packet, part_rest, away_rest, hub_hot, slot_hot, hub_some, slot_some))
    part, hid_hub, hid_slot = call(
        functools.partial(away_body, hubs, STEP2),
        (shape((half, hid), F32), shape((hub_cols, hid), BF16), shape((slot_cols, hid), BF16)),
        got, w_in, hub_mat, sparse_mat,
        flops=products * hid // 2,
    )
    away = swap(part)
    part = call(
        functools.partial(own_body, STEP1), shape((half, hid), F32), hid_hub, hid_slot, hub_mat, sparse_mat,
        flops=products * hid // 2,
    )
    scale = float(1.0 / (slab * nrows) ** 0.5)
    logits, dsec, grad_out = call(
        functools.partial(score_body, scale),
        (shape((classes, half), BF16), shape((hid, half), BF16), shape((classes, hid), F32)),
        part, away, w_out.T, labels.reshape(1, half),
    )
    oth = swap(dsec)
    hub_own, slot_own = call(
        functools.partial(back_own_body, STEP3), (shape((hid, hub_cols), F32), shape((hid, slot_cols), F32)),
        dsec, hub_mat, sparse_mat,
        flops=products * hid // 2,
    )
    count = width + classes
    share = -(-count // (8 * nrows)) * 8
    flat = call(
        functools.partial(back_away_body, hubs, STEP4), shape((nrows, share, hid), BF16),
        hub_own, slot_own, grad_out, oth, got, w_in, hub_mat, sparse_mat,
        scratch=[pltpu.VMEM((hid, width), F32)], flops=products * hid // 2,
    )
    mine = call(sum_body, shape((share, hid), F32), exchange(flat))
    whole = exchange(call(share_body, shape((nrows, share, hid), BF16), mine, swap(mine)))
    grad_in, grad_out = call(parts_body, (shape((width, hid), F32), shape((classes, hid), F32)), whole)
    return (logits.T, grad_in, grad_out.T)


def solution(mesh):
    return jax.shard_map(
        on_device,
        mesh=mesh,
        in_specs=(
            P("rows", None),
            P(),
            P(),
            P(("rows", "rep")),
            P("rows", "rep", None),
            P("rows", "rep", None),
            P("rows", "rep", None),
            P("rows", "rep", None),
        ),
        out_specs=(P(("rows", "rep"), None), P(), P()),
        check_vma=False,
    )
```

```python
import functools
import jax
import jax.numpy as jnp
from jax import lax
from jax.experimental import pallas as pl
from jax.experimental.pallas import tpu as pltpu
from jax.sharding import PartitionSpec as P

SWAP = [(0, 1), (1, 0)]
F32, BF16 = jnp.float32, jnp.bfloat16
VM = pl.BlockSpec(memory_space=pltpu.VMEM)
MIB = 1024 * 1024
PIECES = 1
TOP = 6
STEP1 = 1024
STEP2 = 512
STEP3 = 4096
STEP4 = 2048


def dot(a, b):
    return jnp.dot(a, b, preferred_element_type=F32)


def dot_t(a, b):
    return lax.dot_general(a, b, (((1,), (1,)), ((), ())), preferred_element_type=F32)


def call(body, outs, *args, flops=0, traffic=0, scratch=(), limit=16):
    return pl.pallas_call(
        body,
        out_shape=outs,
        in_specs=[VM] * len(args),
        out_specs=jax.tree.map(lambda _: VM, outs),
        scratch_shapes=scratch,
        compiler_params=pltpu.CompilerParams(vmem_limit_bytes=limit * MIB),
        cost_estimate=pl.CostEstimate(flops=flops, bytes_accessed=traffic, transcendentals=0),
    )(*args)


def one_hot(row, slab):
    count = row.shape[1]
    index = jnp.broadcast_to(row, (128, count)).T
    wide = jnp.concatenate([index] * (slab // 128), axis=1)
    return (wide == lax.broadcasted_iota(jnp.int32, (count, slab), 1)).astype(BF16)


def spread(hub, slot, out_ref):
    peers, rows, width = out_ref.shape
    hubs = hub.shape[0]
    whole = jnp.concatenate(
        [
            jnp.broadcast_to(hub[None], (peers, hubs, width)),
            slot.reshape(peers, rows - hubs, width),
        ],
        axis=1,
    )
    out_ref[...] = whole.astype(BF16)


def pick_body(feat_hbm, hub_hbm, slot_hbm, out_ref, hub_hot, slot_hot, feat_ref, hub_ref, slot_ref, sems):
    slab = feat_ref.shape[0]
    rows = slab // PIECES
    copies = [
        pltpu.make_async_copy(hub_hbm, hub_ref, sems.at[PIECES]),
        pltpu.make_async_copy(slot_hbm, slot_ref, sems.at[PIECES + 1]),
    ]
    for i in range(PIECES):
        at = pl.ds(i * rows, rows)
        copies.append(pltpu.make_async_copy(feat_hbm.at[at], feat_ref.at[at], sems.at[i]))
    for copy in copies:
        copy.start()
    copies[0].wait()
    copies[1].wait()
    hub_hot[...] = one_hot(hub_ref[...], slab)
    slot_hot[...] = one_hot(slot_ref[...], slab)
    hub = slot = 0.0
    for i in range(PIECES):
        at = pl.ds(i * rows, rows)
        copies[2 + i].wait()
        hub += dot(hub_hot[:, at], feat_ref[at, :])
        slot += dot(slot_hot[:, at], feat_ref[at, :])
    spread(hub, slot, out_ref)


def pick(packet, feats, hub_row, slot_row, flops):
    return pl.pallas_call(
        pick_body,
        out_shape=(packet,)
        + tuple(jax.ShapeDtypeStruct((x.shape[1], feats.shape[0]), BF16) for x in (hub_row, slot_row)),
        in_specs=[pl.BlockSpec(memory_space=pl.ANY)] * 3,
        out_specs=(VM, VM, VM),
        scratch_shapes=[pltpu.VMEM(x.shape, x.dtype) for x in (feats, hub_row, slot_row)]
        + [pltpu.SemaphoreType.DMA((PIECES + 2,))],
        compiler_params=pltpu.CompilerParams(vmem_limit_bytes=16 * MIB),
        cost_estimate=pl.CostEstimate(flops=flops, bytes_accessed=0, transcendentals=0),
    )(*(pltpu.with_memory_space_constraint(x, pltpu.HBM) for x in (feats, hub_row, slot_row)))


def pick_top_body(part_ref, away_ref, hub_hot, slot_hot, hub_ref, slot_ref):
    values = (part_ref[...] + away_ref[...]).astype(BF16)
    top = pl.ds(0, values.shape[0])
    hub_ref[...] = dot(hub_hot[:, top], values)
    slot_ref[...] = dot(slot_hot[:, top], values)


def pick_rest_body(part_ref, away_ref, hub_hot, slot_hot, hub_ref, slot_ref, out_ref):
    values = (part_ref[...] + away_ref[...]).astype(BF16)
    count = values.shape[0]
    rest = pl.ds(hub_hot.shape[1] - count, count)
    hub = hub_ref[...] + dot(hub_hot[:, rest], values)
    slot = slot_ref[...] + dot(slot_hot[:, rest], values)
    spread(hub, slot, out_ref)


def split(got_ref, hubs):
    peers, rows, width = got_ref.shape
    hub = got_ref[:, :hubs, :].reshape(peers * hubs, width)
    slot = got_ref[:, hubs:, :].astype(F32).reshape(peers * (rows - hubs), width).astype(BF16)
    return hub, slot


def first_body(hubs, start, got_ref, hub_mat, sparse_mat, part_ref):
    hub, slot = split(got_ref, hubs)
    at = pl.ds(start, part_ref.shape[0])
    part_ref[...] = dot(hub_mat[at, :], hub) + dot(sparse_mat[at, :], slot)


def second_rows(step, start, part_ref, hid_hub, hid_slot, hub_mat, sparse_mat):
    for i in range(part_ref.shape[0] // step):
        at = pl.ds(i * step, step)
        src = pl.ds(pl.multiple_of(start + i * step, step), step)
        part_ref[at, :] = dot(hub_mat[src, :], hid_hub[...]) + dot(sparse_mat[src, :], hid_slot[...])


def away_body(hubs, step, got_ref, w_ref, hub_mat, sparse_mat, part_ref, hid_hub, hid_slot):
    hub, slot = split(got_ref, hubs)
    hid_hub[...] = jnp.maximum(dot(hub, w_ref[...]), 0.0).astype(BF16)
    hid_slot[...] = jnp.maximum(dot(slot, w_ref[...]), 0.0).astype(BF16)
    start = (1 - lax.axis_index("rep")) * part_ref.shape[0]
    second_rows(step, start, part_ref, hid_hub, hid_slot, hub_mat, sparse_mat)


def own_body(step, hid_hub, hid_slot, hub_mat, sparse_mat, part_ref):
    start = lax.axis_index("rep") * part_ref.shape[0]
    second_rows(step, start, part_ref, hid_hub, hid_slot, hub_mat, sparse_mat)


def score_body(scale, part_ref, away_ref, w_ref, label_ref, logit_ref, dsec_ref, grad_ref):
    second = (part_ref[...] + away_ref[...]).astype(BF16)
    scores = dot_t(w_ref[...], second)
    logit_ref[...] = scores.astype(BF16)
    top = jnp.max(scores, axis=0, keepdims=True)
    expo = jnp.exp(scores - top)
    probs = expo / jnp.sum(expo, axis=0, keepdims=True)
    hot = label_ref[...] == lax.broadcasted_iota(jnp.int32, scores.shape, 0)
    dscore = (probs - hot.astype(F32)) * scale
    high = dscore.astype(BF16)
    low = (dscore - high.astype(F32)).astype(BF16)
    grad_ref[...] = dot(high, second) + dot(low, second)
    dsec_ref[...] = lax.dot_general(
        w_ref[...], high, (((0,), (0,)), ((), ())), preferred_element_type=F32
    ).astype(BF16)


def back_own_body(step, dsec_ref, hub_mat, sparse_mat, hub_out, slot_out):
    half = dsec_ref.shape[1]
    src = pl.ds(pl.multiple_of(lax.axis_index("rep") * half, half), half)
    slot_out[...] = dot(dsec_ref[...], sparse_mat[src, :])

    @pl.loop(0, hub_mat.shape[1] // step)
    def _(i):
        at = pl.ds(pl.multiple_of(i * step, step), step)
        hub_out[:, at] = dot(dsec_ref[...], hub_mat[src, at])


def back_away_body(
    hubs, step, hub_own, slot_own, grad_ref, dsec_ref, got_ref, hid_hub, hid_slot, hub_mat, sparse_mat, out_ref, acc_ref
):
    half = dsec_ref.shape[1]
    src = pl.ds(pl.multiple_of((1 - lax.axis_index("rep")) * half, half), half)
    peers, rows, width = got_ref.shape

    def term(cols, mat, own, hid):
        grad = jnp.where(hid.astype(F32).T > 0, dot(dsec_ref[...], mat) + own, 0.0).astype(BF16)
        return dot(grad, cols)

    slot = got_ref[:, hubs:, :].astype(F32).reshape(peers * (rows - hubs), width).astype(BF16)
    acc_ref[...] = term(slot, sparse_mat[src, :], slot_own[...], hid_slot[...])
    group = step // hubs

    total = 0.0
    for i in range(hub_mat.shape[1] // step):
        at = pl.ds(i * step, step)
        cols = got_ref[pl.ds(i * group, group), :hubs, :].reshape(step, width)
        total += term(cols, hub_mat[src, at], hub_own[:, at], hid_hub[at, :])
    acc_ref[...] += total

    classes = grad_ref.shape[0]
    rest = out_ref.shape[0] * out_ref.shape[1] - width - classes
    flat = jnp.concatenate([acc_ref[...].T, grad_ref[...], jnp.zeros((rest, out_ref.shape[2]), F32)], axis=0)
    out_ref[...] = flat.reshape(out_ref.shape).astype(BF16)


def sum_body(got_ref, out_ref):
    out_ref[...] = jnp.sum(got_ref[...].astype(F32), axis=0)


def share_body(mine_ref, away_ref, out_ref):
    mine = (mine_ref[...] + away_ref[...]).astype(BF16).astype(F32)
    out_ref[...] = jnp.broadcast_to(mine[None], out_ref.shape).astype(BF16)


def parts_body(got_ref, in_ref, out_ref):
    peers, rows, width = got_ref.shape
    whole = got_ref[...].astype(F32).reshape(peers * rows, width)
    first, second = in_ref.shape[0], out_ref.shape[0]
    in_ref[...] = whole[:first]
    out_ref[...] = whole[first : first + second]


def on_device(node_feats, w_in, w_out, labels, hub_rows, send_rows, adj_hub, adj_sparse):
    nrows = lax.axis_size("rows")
    slab, width = node_feats.shape
    half = slab // lax.axis_size("rep")
    hid, classes = w_out.shape
    hubs = hub_rows.shape[2]
    slots = send_rows.shape[2] // nrows
    hub_cols, slot_cols = nrows * hubs, nrows * slots
    hub_row = hub_rows.reshape(1, hubs)
    slot_row = send_rows.reshape(1, slot_cols)
    hub_mat = pltpu.with_memory_space_constraint(adj_hub.reshape(slab, hub_cols), pltpu.VMEM)
    sparse_mat = pltpu.with_memory_space_constraint(adj_sparse.reshape(slab, slot_cols), pltpu.VMEM)
    shape = jax.ShapeDtypeStruct
    packet = shape((nrows, hubs + slots, width), BF16)
    products = 2 * slab * (hub_cols + slot_cols)

    def exchange(x):
        return lax.all_to_all(x, "rows", split_axis=0, concat_axis=0, tiled=True)

    def swap(x):
        return lax.ppermute(x, "rep", SWAP)

    sent, hub_hot, slot_hot = pick(packet, node_feats, hub_row, slot_row, products * 256)
    got = exchange(sent)

    def first_rows(start, rows):
        return call(
            functools.partial(first_body, hubs, start), shape((rows, width), F32), got, hub_mat, sparse_mat,
            flops=products * rows // slab * width * 2,
        )

    top = slab * TOP // 8
    part = first_rows(0, top)
    away = swap(part)
    part_rest = first_rows(top, slab - top)
    away_rest = swap(part_rest)
    hub_some, slot_some = call(
        pick_top_body, (shape((hubs, width), F32), shape((slot_cols, width), F32)), part, away, hub_hot, slot_hot,
        flops=2 * (hubs + slot_cols) * slab * width,
    )
    got = exchange(call(pick_rest_body, packet, part_rest, away_rest, hub_hot, slot_hot, hub_some, slot_some))
    part, hid_hub, hid_slot = call(
        functools.partial(away_body, hubs, STEP2),
        (shape((half, hid), F32), shape((hub_cols, hid), BF16), shape((slot_cols, hid), BF16)),
        got, w_in, hub_mat, sparse_mat,
        flops=products * hid // 2,
    )
    away = swap(part)
    part = call(
        functools.partial(own_body, STEP1), shape((half, hid), F32), hid_hub, hid_slot, hub_mat, sparse_mat,
        flops=products * hid // 2,
    )
    scale = float(1.0 / (slab * nrows) ** 0.5)
    logits, dsec, grad_out = call(
        functools.partial(score_body, scale),
        (shape((classes, half), BF16), shape((hid, half), BF16), shape((classes, hid), F32)),
        part, away, w_out.T, labels.reshape(1, half),
    )
    oth = swap(dsec)
    hub_own, slot_own = call(
        functools.partial(back_own_body, STEP3), (shape((hid, hub_cols), F32), shape((hid, slot_cols), F32)),
        dsec, hub_mat, sparse_mat,
        flops=products * hid // 2,
    )
    count = width + classes
    share = -(-count // (8 * nrows)) * 8
    flat = call(
        functools.partial(back_away_body, hubs, STEP4), shape((nrows, share, hid), BF16),
        hub_own, slot_own, grad_out, oth, got, hid_hub, hid_slot, hub_mat, sparse_mat,
        scratch=[pltpu.VMEM((hid, width), F32)], flops=products * hid // 2,
    )
    mine = call(sum_body, shape((share, hid), F32), exchange(flat))
    whole = exchange(call(share_body, shape((nrows, share, hid), BF16), mine, swap(mine)))
    grad_in, grad_out = call(parts_body, (shape((width, hid), F32), shape((classes, hid), F32)), whole)
    return (logits.T, grad_in, grad_out.T)


def solution(mesh):
    return jax.shard_map(
        on_device,
        mesh=mesh,
        in_specs=(
            P("rows", None),
            P(),
            P(),
            P(("rows", "rep")),
            P("rows", "rep", None),
            P("rows", "rep", None),
            P("rows", "rep", None),
            P("rows", "rep", None),
        ),
        out_specs=(P(("rows", "rep"), None), P(), P()),
        check_vma=False,
    )
```

```python
import functools
import jax
import jax.numpy as jnp
from jax import lax
from jax.experimental import pallas as pl
from jax.experimental.pallas import tpu as pltpu
from jax.sharding import Mesh
from jax.sharding import PartitionSpec as P

SWAP = [(0, 1), (1, 0)]
ROWS = ("z", "x", "y")
NEAR, FAR = ("y", "rep"), ("z", "x")
F32, BF16 = jnp.float32, jnp.bfloat16
VM = pl.BlockSpec(memory_space=pltpu.VMEM)
MIB = 1024 * 1024
PIECES = 1
TOP = 6
STEP1 = 1024
STEP2 = 512
STEP3 = 4096
STEP4 = 2048


def dot(a, b):
    return jnp.dot(a, b, preferred_element_type=F32)


def dot_t(a, b):
    return lax.dot_general(a, b, (((1,), (1,)), ((), ())), preferred_element_type=F32)


def call(body, outs, *args, flops=0, traffic=0, scratch=(), limit=16):
    return pl.pallas_call(
        body,
        out_shape=outs,
        in_specs=[VM] * len(args),
        out_specs=jax.tree.map(lambda _: VM, outs),
        scratch_shapes=scratch,
        compiler_params=pltpu.CompilerParams(vmem_limit_bytes=limit * MIB),
        cost_estimate=pl.CostEstimate(flops=flops, bytes_accessed=traffic, transcendentals=0),
    )(*args)


def one_hot(row, slab):
    count = row.shape[1]
    index = jnp.broadcast_to(row, (128, count)).T
    wide = jnp.concatenate([index] * (slab // 128), axis=1)
    return (wide == lax.broadcasted_iota(jnp.int32, (count, slab), 1)).astype(BF16)


def spread(hub, slot, out_ref):
    peers, rows, width = out_ref.shape
    hubs = hub.shape[0]
    whole = jnp.concatenate(
        [
            jnp.broadcast_to(hub[None], (peers, hubs, width)),
            slot.reshape(peers, rows - hubs, width),
        ],
        axis=1,
    )
    out_ref[...] = whole.astype(BF16)


def pick_body(feat_hbm, hub_hbm, slot_hbm, out_ref, hub_hot, slot_hot, feat_ref, hub_ref, slot_ref, sems):
    slab = feat_ref.shape[0]
    rows = slab // PIECES
    copies = [
        pltpu.make_async_copy(hub_hbm, hub_ref, sems.at[PIECES]),
        pltpu.make_async_copy(slot_hbm, slot_ref, sems.at[PIECES + 1]),
    ]
    for i in range(PIECES):
        at = pl.ds(i * rows, rows)
        copies.append(pltpu.make_async_copy(feat_hbm.at[at], feat_ref.at[at], sems.at[i]))
    for copy in copies:
        copy.start()
    copies[0].wait()
    copies[1].wait()
    hub_hot[...] = one_hot(hub_ref[...], slab)
    slot_hot[...] = one_hot(slot_ref[...], slab)
    hub = slot = 0.0
    for i in range(PIECES):
        at = pl.ds(i * rows, rows)
        copies[2 + i].wait()
        hub += dot(hub_hot[:, at], feat_ref[at, :])
        slot += dot(slot_hot[:, at], feat_ref[at, :])
    spread(hub, slot, out_ref)


def pick(packet, feats, hub_row, slot_row, flops):
    return pl.pallas_call(
        pick_body,
        out_shape=(packet,)
        + tuple(jax.ShapeDtypeStruct((x.shape[1], feats.shape[0]), BF16) for x in (hub_row, slot_row)),
        in_specs=[pl.BlockSpec(memory_space=pl.ANY)] * 3,
        out_specs=(VM, VM, VM),
        scratch_shapes=[pltpu.VMEM(x.shape, x.dtype) for x in (feats, hub_row, slot_row)]
        + [pltpu.SemaphoreType.DMA((PIECES + 2,))],
        compiler_params=pltpu.CompilerParams(vmem_limit_bytes=16 * MIB),
        cost_estimate=pl.CostEstimate(flops=flops, bytes_accessed=0, transcendentals=0),
    )(*(pltpu.with_memory_space_constraint(x, pltpu.HBM) for x in (feats, hub_row, slot_row)))


def pick_top_body(part_ref, away_ref, hub_hot, slot_hot, hub_ref, slot_ref):
    values = (part_ref[...] + away_ref[...]).astype(BF16)
    top = pl.ds(0, values.shape[0])
    hub_ref[...] = dot(hub_hot[:, top], values)
    slot_ref[...] = dot(slot_hot[:, top], values)


def pick_rest_body(part_ref, away_ref, hub_hot, slot_hot, hub_ref, slot_ref, out_ref):
    values = (part_ref[...] + away_ref[...]).astype(BF16)
    count = values.shape[0]
    rest = pl.ds(hub_hot.shape[1] - count, count)
    hub = hub_ref[...] + dot(hub_hot[:, rest], values)
    slot = slot_ref[...] + dot(slot_hot[:, rest], values)
    spread(hub, slot, out_ref)


def split(got_ref, hubs):
    peers, rows, width = got_ref.shape
    hub = got_ref[:, :hubs, :].reshape(peers * hubs, width)
    slot = got_ref[:, hubs:, :].astype(F32).reshape(peers * (rows - hubs), width).astype(BF16)
    return hub, slot


def first_body(hubs, start, got_ref, hub_mat, sparse_mat, part_ref):
    hub, slot = split(got_ref, hubs)
    at = pl.ds(start, part_ref.shape[0])
    part_ref[...] = dot(hub_mat[at, :], hub) + dot(sparse_mat[at, :], slot)


def second_rows(step, start, part_ref, hid_hub, hid_slot, hub_mat, sparse_mat):
    for i in range(part_ref.shape[0] // step):
        at = pl.ds(i * step, step)
        src = pl.ds(pl.multiple_of(start + i * step, step), step)
        part_ref[at, :] = dot(hub_mat[src, :], hid_hub[...]) + dot(sparse_mat[src, :], hid_slot[...])


def away_body(hubs, step, got_ref, w_ref, hub_mat, sparse_mat, part_ref, hid_hub, hid_slot):
    hub, slot = split(got_ref, hubs)
    hid_hub[...] = jnp.maximum(dot(hub, w_ref[...]), 0.0).astype(BF16)
    hid_slot[...] = jnp.maximum(dot(slot, w_ref[...]), 0.0).astype(BF16)
    start = (1 - lax.axis_index("rep")) * part_ref.shape[0]
    second_rows(step, start, part_ref, hid_hub, hid_slot, hub_mat, sparse_mat)


def own_body(step, hid_hub, hid_slot, hub_mat, sparse_mat, part_ref):
    start = lax.axis_index("rep") * part_ref.shape[0]
    second_rows(step, start, part_ref, hid_hub, hid_slot, hub_mat, sparse_mat)


def score_body(scale, part_ref, away_ref, w_ref, label_ref, logit_ref, dsec_ref, grad_ref):
    second = (part_ref[...] + away_ref[...]).astype(BF16)
    scores = dot_t(w_ref[...], second)
    logit_ref[...] = scores.astype(BF16)
    top = jnp.max(scores, axis=0, keepdims=True)
    expo = jnp.exp(scores - top)
    probs = expo / jnp.sum(expo, axis=0, keepdims=True)
    hot = label_ref[...] == lax.broadcasted_iota(jnp.int32, scores.shape, 0)
    dscore = (probs - hot.astype(F32)) * scale
    high = dscore.astype(BF16)
    low = (dscore - high.astype(F32)).astype(BF16)
    grad_ref[...] = dot(high, second) + dot(low, second)
    dsec_ref[...] = lax.dot_general(
        w_ref[...], high, (((0,), (0,)), ((), ())), preferred_element_type=F32
    ).astype(BF16)


def back_own_body(step, dsec_ref, hub_mat, sparse_mat, hub_out, slot_out):
    half = dsec_ref.shape[1]
    src = pl.ds(pl.multiple_of(lax.axis_index("rep") * half, half), half)
    slot_out[...] = dot(dsec_ref[...], sparse_mat[src, :])

    @pl.loop(0, hub_mat.shape[1] // step)
    def _(i):
        at = pl.ds(pl.multiple_of(i * step, step), step)
        hub_out[:, at] = dot(dsec_ref[...], hub_mat[src, at])


def back_away_body(
    hubs, step, hub_own, slot_own, grad_ref, dsec_ref, got_ref, hid_hub, hid_slot, hub_mat, sparse_mat, out_ref, acc_ref
):
    half = dsec_ref.shape[1]
    src = pl.ds(pl.multiple_of((1 - lax.axis_index("rep")) * half, half), half)
    peers, rows, width = got_ref.shape

    def term(cols, mat, own, hid):
        grad = jnp.where(hid.astype(F32).T > 0, dot(dsec_ref[...], mat) + own, 0.0).astype(BF16)
        return dot(grad, cols)

    slot = got_ref[:, hubs:, :].astype(F32).reshape(peers * (rows - hubs), width).astype(BF16)
    acc_ref[...] = term(slot, sparse_mat[src, :], slot_own[...], hid_slot[...])
    group = step // hubs

    total = 0.0
    for i in range(hub_mat.shape[1] // step):
        at = pl.ds(i * step, step)
        cols = got_ref[pl.ds(i * group, group), :hubs, :].reshape(step, width)
        total += term(cols, hub_mat[src, at], hub_own[:, at], hid_hub[at, :])
    acc_ref[...] += total

    classes = grad_ref.shape[0]
    rest = out_ref.shape[0] * out_ref.shape[1] - width - classes
    flat = jnp.concatenate([acc_ref[...].T, grad_ref[...], jnp.zeros((rest, out_ref.shape[2]), F32)], axis=0)
    out_ref[...] = flat.reshape(out_ref.shape).astype(BF16)


def fold_body(got_ref, out_ref):
    total = jnp.sum(got_ref[...].astype(F32), axis=0).astype(BF16).astype(F32)
    out_ref[...] = jnp.broadcast_to(total[None], out_ref.shape).astype(BF16)


def parts_body(got_ref, in_ref, out_ref):
    peers, rows, width = got_ref.shape
    whole = got_ref[...].astype(F32).reshape(peers * rows, width)
    first, second = in_ref.shape[0], out_ref.shape[0]
    in_ref[...] = whole[:first]
    out_ref[...] = whole[first : first + second]


def on_device(node_feats, w_in, w_out, labels, hub_rows, send_rows, adj_hub, adj_sparse):
    nrows = lax.axis_size(ROWS)
    slab, width = node_feats.shape
    half = slab // lax.axis_size("rep")
    hid, classes = w_out.shape
    hubs = hub_rows.shape[2]
    slots = send_rows.shape[2] // nrows
    hub_cols, slot_cols = nrows * hubs, nrows * slots
    hub_row = hub_rows.reshape(1, hubs)
    slot_row = send_rows.reshape(1, slot_cols)
    hub_mat = pltpu.with_memory_space_constraint(adj_hub.reshape(slab, hub_cols), pltpu.VMEM)
    sparse_mat = pltpu.with_memory_space_constraint(adj_sparse.reshape(slab, slot_cols), pltpu.VMEM)
    shape = jax.ShapeDtypeStruct
    packet = shape((nrows, hubs + slots, width), BF16)
    products = 2 * slab * (hub_cols + slot_cols)

    def exchange(x, axes=ROWS):
        return lax.all_to_all(x, axes, split_axis=0, concat_axis=0, tiled=True)

    def swap(x):
        return lax.ppermute(x, "rep", SWAP)

    sent, hub_hot, slot_hot = pick(packet, node_feats, hub_row, slot_row, products * 256)
    got = exchange(sent)

    def first_rows(start, rows):
        return call(
            functools.partial(first_body, hubs, start), shape((rows, width), F32), got, hub_mat, sparse_mat,
            flops=products * rows // slab * width * 2,
        )

    top = slab * TOP // 8
    part = first_rows(0, top)
    away = swap(part)
    part_rest = first_rows(top, slab - top)
    away_rest = swap(part_rest)
    hub_some, slot_some = call(
        pick_top_body, (shape((hubs, width), F32), shape((slot_cols, width), F32)), part, away, hub_hot, slot_hot,
        flops=2 * (hubs + slot_cols) * slab * width,
    )
    got = exchange(call(pick_rest_body, packet, part_rest, away_rest, hub_hot, slot_hot, hub_some, slot_some))
    part, hid_hub, hid_slot = call(
        functools.partial(away_body, hubs, STEP2),
        (shape((half, hid), F32), shape((hub_cols, hid), BF16), shape((slot_cols, hid), BF16)),
        got, w_in, hub_mat, sparse_mat,
        flops=products * hid // 2,
    )
    away = swap(part)
    part = call(
        functools.partial(own_body, STEP1), shape((half, hid), F32), hid_hub, hid_slot, hub_mat, sparse_mat,
        flops=products * hid // 2,
    )
    scale = float(1.0 / (slab * nrows) ** 0.5)
    logits, dsec, grad_out = call(
        functools.partial(score_body, scale),
        (shape((classes, half), BF16), shape((hid, half), BF16), shape((classes, hid), F32)),
        part, away, w_out.T, labels.reshape(1, half),
    )
    oth = swap(dsec)
    hub_own, slot_own = call(
        functools.partial(back_own_body, STEP3), (shape((hid, hub_cols), F32), shape((hid, slot_cols), F32)),
        dsec, hub_mat, sparse_mat,
        flops=products * hid // 2,
    )
    count = width + classes
    near, far = lax.axis_size(NEAR), lax.axis_size(FAR)
    share = -(-count // (8 * near)) * 8
    flat = call(
        functools.partial(back_away_body, hubs, STEP4), shape((near, share, hid), BF16),
        hub_own, slot_own, grad_out, oth, got, hid_hub, hid_slot, hub_mat, sparse_mat,
        scratch=[pltpu.VMEM((hid, width), F32)], flops=products * hid // 2,
    )
    piece = call(fold_body, shape((far, share, hid), BF16), exchange(flat, NEAR))
    whole = exchange(call(fold_body, shape((near, share, hid), BF16), exchange(piece, FAR)), NEAR)
    grad_in, grad_out = call(parts_body, (shape((width, hid), F32), shape((classes, hid), F32)), whole)
    return (logits.T, grad_in, grad_out.T)


def solution(mesh):
    rows, cores = mesh.devices.shape
    side = round(rows ** (1 / 3))
    cube = Mesh(mesh.devices.reshape(-1, side, side, cores), ("z", "x", "y", "rep"))
    return jax.shard_map(
        on_device,
        mesh=cube,
        in_specs=(
            P(ROWS, None),
            P(),
            P(),
            P((*ROWS, "rep")),
            P(ROWS, "rep", None),
            P(ROWS, "rep", None),
            P(ROWS, "rep", None),
            P(ROWS, "rep", None),
        ),
        out_specs=(P((*ROWS, "rep"), None), P(), P()),
        check_vma=False,
    )
```

```python
import functools
import jax
import jax.numpy as jnp
from jax import lax
from jax.experimental import pallas as pl
from jax.experimental.pallas import tpu as pltpu
from jax.sharding import Mesh
from jax.sharding import PartitionSpec as P

SWAP = [(0, 1), (1, 0)]
ROWS = ("z", "x", "y")
NEAR, FAR = ("y", "rep"), ("z", "x")
F32, BF16 = jnp.float32, jnp.bfloat16
VM = pl.BlockSpec(memory_space=pltpu.VMEM)
MIB = 1024 * 1024
PIECES = 1
TOP = 6
STEP1 = 256
STEP2 = 256
STEP3 = 4096
STEP4 = 2048


def dot(a, b):
    return jnp.dot(a, b, preferred_element_type=F32)


def dot_t(a, b):
    return lax.dot_general(a, b, (((1,), (1,)), ((), ())), preferred_element_type=F32)


def call(body, outs, *args, flops=0, traffic=0, scratch=(), limit=16):
    return pl.pallas_call(
        body,
        out_shape=outs,
        in_specs=[VM] * len(args),
        out_specs=jax.tree.map(lambda _: VM, outs),
        scratch_shapes=scratch,
        compiler_params=pltpu.CompilerParams(vmem_limit_bytes=limit * MIB),
        cost_estimate=pl.CostEstimate(flops=flops, bytes_accessed=traffic, transcendentals=0),
    )(*args)


def one_hot(row, slab):
    count = row.shape[1]
    index = jnp.broadcast_to(row, (128, count)).T
    wide = jnp.concatenate([index] * (slab // 128), axis=1)
    return (wide == lax.broadcasted_iota(jnp.int32, (count, slab), 1)).astype(BF16)


def spread(hub, slot, out_ref):
    peers, rows, width = out_ref.shape
    hubs = hub.shape[0]
    whole = jnp.concatenate(
        [
            jnp.broadcast_to(hub[None], (peers, hubs, width)),
            slot.reshape(peers, rows - hubs, width),
        ],
        axis=1,
    )
    out_ref[...] = whole.astype(BF16)


def pick_body(feat_hbm, hub_hbm, slot_hbm, out_ref, hub_hot, slot_hot, feat_ref, hub_ref, slot_ref, sems):
    slab = feat_ref.shape[0]
    rows = slab // PIECES
    copies = [
        pltpu.make_async_copy(hub_hbm, hub_ref, sems.at[PIECES]),
        pltpu.make_async_copy(slot_hbm, slot_ref, sems.at[PIECES + 1]),
    ]
    for i in range(PIECES):
        at = pl.ds(i * rows, rows)
        copies.append(pltpu.make_async_copy(feat_hbm.at[at], feat_ref.at[at], sems.at[i]))
    for copy in copies:
        copy.start()
    copies[0].wait()
    copies[1].wait()
    hub_hot[...] = one_hot(hub_ref[...], slab)
    slot_hot[...] = one_hot(slot_ref[...], slab)
    hub = slot = 0.0
    for i in range(PIECES):
        at = pl.ds(i * rows, rows)
        copies[2 + i].wait()
        hub += dot(hub_hot[:, at], feat_ref[at, :])
        slot += dot(slot_hot[:, at], feat_ref[at, :])
    spread(hub, slot, out_ref)


def pick(packet, feats, hub_row, slot_row, flops):
    return pl.pallas_call(
        pick_body,
        out_shape=(packet,)
        + tuple(jax.ShapeDtypeStruct((x.shape[1], feats.shape[0]), BF16) for x in (hub_row, slot_row)),
        in_specs=[pl.BlockSpec(memory_space=pl.ANY)] * 3,
        out_specs=(VM, VM, VM),
        scratch_shapes=[pltpu.VMEM(x.shape, x.dtype) for x in (feats, hub_row, slot_row)]
        + [pltpu.SemaphoreType.DMA((PIECES + 2,))],
        compiler_params=pltpu.CompilerParams(vmem_limit_bytes=16 * MIB),
        cost_estimate=pl.CostEstimate(flops=flops, bytes_accessed=0, transcendentals=0),
    )(*(pltpu.with_memory_space_constraint(x, pltpu.HBM) for x in (feats, hub_row, slot_row)))


def pick_top_body(part_ref, away_ref, hub_hot, slot_hot, hub_ref, slot_ref):
    values = (part_ref[...] + away_ref[...]).astype(BF16)
    top = pl.ds(0, values.shape[0])
    hub_ref[...] = dot(hub_hot[:, top], values)
    slot_ref[...] = dot(slot_hot[:, top], values)


def pick_rest_body(part_ref, away_ref, hub_hot, slot_hot, hub_ref, slot_ref, out_ref):
    values = (part_ref[...] + away_ref[...]).astype(BF16)
    count = values.shape[0]
    rest = pl.ds(hub_hot.shape[1] - count, count)
    hub = hub_ref[...] + dot(hub_hot[:, rest], values)
    slot = slot_ref[...] + dot(slot_hot[:, rest], values)
    spread(hub, slot, out_ref)


def split(got_ref, hubs):
    peers, rows, width = got_ref.shape
    hub = got_ref[:, :hubs, :].reshape(peers * hubs, width)
    slot = got_ref[:, hubs:, :].astype(F32).reshape(peers * (rows - hubs), width).astype(BF16)
    return hub, slot


def first_body(hubs, start, got_ref, hub_mat, sparse_mat, part_ref):
    hub, slot = split(got_ref, hubs)
    at = pl.ds(start, part_ref.shape[0])
    part_ref[...] = dot(hub_mat[at, :], hub) + dot(sparse_mat[at, :], slot)


def second_rows(step, start, part_ref, hid_hub, hid_slot, hub_mat, sparse_mat):
    for i in range(part_ref.shape[0] // step):
        at = pl.ds(i * step, step)
        src = pl.ds(pl.multiple_of(start + i * step, step), step)
        part_ref[at, :] = dot(hub_mat[src, :], hid_hub[...]) + dot(sparse_mat[src, :], hid_slot[...])


def away_body(hubs, step, got_ref, w_ref, hub_mat, sparse_mat, part_ref, hid_hub, hid_slot):
    hub, slot = split(got_ref, hubs)
    hid_hub[...] = jnp.maximum(dot(hub, w_ref[...]), 0.0).astype(BF16)
    hid_slot[...] = jnp.maximum(dot(slot, w_ref[...]), 0.0).astype(BF16)
    start = (1 - lax.axis_index("rep")) * part_ref.shape[0]
    second_rows(step, start, part_ref, hid_hub, hid_slot, hub_mat, sparse_mat)


def own_body(step, hid_hub, hid_slot, hub_mat, sparse_mat, part_ref):
    start = lax.axis_index("rep") * part_ref.shape[0]
    second_rows(step, start, part_ref, hid_hub, hid_slot, hub_mat, sparse_mat)


def score_body(scale, part_ref, away_ref, w_ref, label_ref, logit_ref, dsec_ref, grad_ref):
    second = (part_ref[...] + away_ref[...]).astype(BF16)
    scores = dot_t(w_ref[...], second)
    logit_ref[...] = scores.astype(BF16)
    top = jnp.max(scores, axis=0, keepdims=True)
    expo = jnp.exp(scores - top)
    probs = expo / jnp.sum(expo, axis=0, keepdims=True)
    hot = label_ref[...] == lax.broadcasted_iota(jnp.int32, scores.shape, 0)
    dscore = (probs - hot.astype(F32)) * scale
    high = dscore.astype(BF16)
    low = (dscore - high.astype(F32)).astype(BF16)
    grad_ref[...] = dot(high, second) + dot(low, second)
    dsec_ref[...] = lax.dot_general(
        w_ref[...], high, (((0,), (0,)), ((), ())), preferred_element_type=F32
    ).astype(BF16)


def back_own_body(step, dsec_ref, hub_mat, sparse_mat, hub_out, slot_out):
    half = dsec_ref.shape[1]
    src = pl.ds(pl.multiple_of(lax.axis_index("rep") * half, half), half)
    slot_out[...] = dot(dsec_ref[...], sparse_mat[src, :])

    @pl.loop(0, hub_mat.shape[1] // step)
    def _(i):
        at = pl.ds(pl.multiple_of(i * step, step), step)
        hub_out[:, at] = dot(dsec_ref[...], hub_mat[src, at])


def back_away_body(
    hubs, step, hub_own, slot_own, grad_ref, dsec_ref, got_ref, hid_hub, hid_slot, hub_mat, sparse_mat, out_ref, acc_ref
):
    half = dsec_ref.shape[1]
    src = pl.ds(pl.multiple_of((1 - lax.axis_index("rep")) * half, half), half)
    peers, rows, width = got_ref.shape

    def term(cols, mat, own, hid):
        grad = jnp.where(hid.astype(F32).T > 0, dot(dsec_ref[...], mat) + own, 0.0).astype(BF16)
        return dot(grad, cols)

    slot = got_ref[:, hubs:, :].astype(F32).reshape(peers * (rows - hubs), width).astype(BF16)
    acc_ref[...] = term(slot, sparse_mat[src, :], slot_own[...], hid_slot[...])
    group = step // hubs

    total = 0.0
    for i in range(hub_mat.shape[1] // step):
        at = pl.ds(i * step, step)
        cols = got_ref[pl.ds(i * group, group), :hubs, :].reshape(step, width)
        total += term(cols, hub_mat[src, at], hub_own[:, at], hid_hub[at, :])
    acc_ref[...] += total

    classes = grad_ref.shape[0]
    rest = out_ref.shape[0] * out_ref.shape[1] - width - classes
    flat = jnp.concatenate([acc_ref[...].T, grad_ref[...], jnp.zeros((rest, out_ref.shape[2]), F32)], axis=0)
    out_ref[...] = flat.reshape(out_ref.shape).astype(BF16)


def fold_body(got_ref, out_ref):
    total = jnp.sum(got_ref[...].astype(F32), axis=0).astype(BF16).astype(F32)
    out_ref[...] = jnp.broadcast_to(total[None], out_ref.shape).astype(BF16)


def parts_body(got_ref, in_ref, out_ref):
    peers, rows, width = got_ref.shape
    whole = got_ref[...].astype(F32).reshape(peers * rows, width)
    first, second = in_ref.shape[0], out_ref.shape[0]
    in_ref[...] = whole[:first]
    out_ref[...] = whole[first : first + second]


def on_device(node_feats, w_in, w_out, labels, hub_rows, send_rows, adj_hub, adj_sparse):
    nrows = lax.axis_size(ROWS)
    slab, width = node_feats.shape
    half = slab // lax.axis_size("rep")
    hid, classes = w_out.shape
    hubs = hub_rows.shape[2]
    slots = send_rows.shape[2] // nrows
    hub_cols, slot_cols = nrows * hubs, nrows * slots
    hub_row = hub_rows.reshape(1, hubs)
    slot_row = send_rows.reshape(1, slot_cols)
    hub_mat = pltpu.with_memory_space_constraint(adj_hub.reshape(slab, hub_cols), pltpu.VMEM)
    sparse_mat = pltpu.with_memory_space_constraint(adj_sparse.reshape(slab, slot_cols), pltpu.VMEM)
    shape = jax.ShapeDtypeStruct
    packet = shape((nrows, hubs + slots, width), BF16)
    products = 2 * slab * (hub_cols + slot_cols)

    def exchange(x, axes=ROWS):
        return lax.all_to_all(x, axes, split_axis=0, concat_axis=0, tiled=True)

    def swap(x):
        return lax.ppermute(x, "rep", SWAP)

    sent, hub_hot, slot_hot = pick(packet, node_feats, hub_row, slot_row, products * 256)
    got = exchange(sent)

    def first_rows(start, rows):
        return call(
            functools.partial(first_body, hubs, start), shape((rows, width), F32), got, hub_mat, sparse_mat,
            flops=products * rows // slab * width * 2,
        )

    top = slab * TOP // 8
    part = first_rows(0, top)
    away = swap(part)
    part_rest = first_rows(top, slab - top)
    away_rest = swap(part_rest)
    hub_some, slot_some = call(
        pick_top_body, (shape((hubs, width), F32), shape((slot_cols, width), F32)), part, away, hub_hot, slot_hot,
        flops=2 * (hubs + slot_cols) * slab * width,
    )
    got = exchange(call(pick_rest_body, packet, part_rest, away_rest, hub_hot, slot_hot, hub_some, slot_some))
    part, hid_hub, hid_slot = call(
        functools.partial(away_body, hubs, STEP2),
        (shape((half, hid), F32), shape((hub_cols, hid), BF16), shape((slot_cols, hid), BF16)),
        got, w_in, hub_mat, sparse_mat,
        flops=products * hid // 2,
    )
    away = swap(part)
    part = call(
        functools.partial(own_body, STEP1), shape((half, hid), F32), hid_hub, hid_slot, hub_mat, sparse_mat,
        flops=products * hid // 2,
    )
    scale = float(1.0 / (slab * nrows) ** 0.5)
    logits, dsec, grad_out = call(
        functools.partial(score_body, scale),
        (shape((classes, half), BF16), shape((hid, half), BF16), shape((classes, hid), F32)),
        part, away, w_out.T, labels.reshape(1, half),
    )
    oth = swap(dsec)
    hub_own, slot_own = call(
        functools.partial(back_own_body, STEP3), (shape((hid, hub_cols), F32), shape((hid, slot_cols), F32)),
        dsec, hub_mat, sparse_mat,
        flops=products * hid // 2,
    )
    count = width + classes
    near, far = lax.axis_size(NEAR), lax.axis_size(FAR)
    share = -(-count // (8 * near)) * 8
    flat = call(
        functools.partial(back_away_body, hubs, STEP4), shape((near, share, hid), BF16),
        hub_own, slot_own, grad_out, oth, got, hid_hub, hid_slot, hub_mat, sparse_mat,
        scratch=[pltpu.VMEM((hid, width), F32)], flops=products * hid // 2,
    )
    piece = call(fold_body, shape((far, share, hid), BF16), exchange(flat, NEAR))
    whole = exchange(call(fold_body, shape((near, share, hid), BF16), exchange(piece, FAR)), NEAR)
    grad_in, grad_out = call(parts_body, (shape((width, hid), F32), shape((classes, hid), F32)), whole)
    return (logits.T, grad_in, grad_out.T)


def solution(mesh):
    rows, cores = mesh.devices.shape
    side = round(rows ** (1 / 3))
    cube = Mesh(mesh.devices.reshape(-1, side, side, cores), ("z", "x", "y", "rep"))
    return jax.shard_map(
        on_device,
        mesh=cube,
        in_specs=(
            P(ROWS, None),
            P(),
            P(),
            P((*ROWS, "rep")),
            P(ROWS, "rep", None),
            P(ROWS, "rep", None),
            P(ROWS, "rep", None),
            P(ROWS, "rep", None),
        ),
        out_specs=(P((*ROWS, "rep"), None), P(), P()),
        check_vma=False,
    )
```

```python
import functools
import jax
import jax.numpy as jnp
from jax import lax
from jax.experimental import pallas as pl
from jax.experimental.pallas import tpu as pltpu
from jax.sharding import Mesh
from jax.sharding import PartitionSpec as P

SWAP = [(0, 1), (1, 0)]
ROWS = ("z", "x", "y")
NEAR, FAR = ("y", "rep"), ("z", "x")
F32, BF16 = jnp.float32, jnp.bfloat16
VM = pl.BlockSpec(memory_space=pltpu.VMEM)
MIB = 1024 * 1024
PIECES = 1
TOP = 6
STEP1 = 256
STEP2 = 256
STEP3 = 4096
STEP4 = 2048


def dot(a, b):
    return jnp.dot(a, b, preferred_element_type=F32)


def dot_t(a, b):
    return lax.dot_general(a, b, (((1,), (1,)), ((), ())), preferred_element_type=F32)


def call(body, outs, *args, flops=0, traffic=0, scratch=(), limit=16):
    return pl.pallas_call(
        body,
        out_shape=outs,
        in_specs=[VM] * len(args),
        out_specs=jax.tree.map(lambda _: VM, outs),
        scratch_shapes=scratch,
        compiler_params=pltpu.CompilerParams(vmem_limit_bytes=limit * MIB),
        cost_estimate=pl.CostEstimate(flops=flops, bytes_accessed=traffic, transcendentals=0),
    )(*args)


def one_hot(row, slab):
    count = row.shape[1]
    index = jnp.broadcast_to(row, (128, count)).T
    wide = jnp.concatenate([index] * (slab // 128), axis=1)
    return (wide == lax.broadcasted_iota(jnp.int32, (count, slab), 1)).astype(BF16)


def spread(hub, slot, out_ref):
    peers, rows, width = out_ref.shape
    hubs = hub.shape[0]
    whole = jnp.concatenate(
        [
            jnp.broadcast_to(hub[None], (peers, hubs, width)),
            slot.reshape(peers, rows - hubs, width),
        ],
        axis=1,
    )
    out_ref[...] = whole.astype(BF16)


def pick_body(feat_hbm, hub_hbm, slot_hbm, out_ref, hub_hot, slot_hot, feat_ref, hub_ref, slot_ref, sems):
    slab = feat_ref.shape[0]
    rows = slab // PIECES
    copies = [
        pltpu.make_async_copy(hub_hbm, hub_ref, sems.at[PIECES]),
        pltpu.make_async_copy(slot_hbm, slot_ref, sems.at[PIECES + 1]),
    ]
    for i in range(PIECES):
        at = pl.ds(i * rows, rows)
        copies.append(pltpu.make_async_copy(feat_hbm.at[at], feat_ref.at[at], sems.at[i]))
    for copy in copies:
        copy.start()
    copies[0].wait()
    copies[1].wait()
    hub_hot[...] = one_hot(hub_ref[...], slab)
    slot_hot[...] = one_hot(slot_ref[...], slab)
    hub = slot = 0.0
    for i in range(PIECES):
        at = pl.ds(i * rows, rows)
        copies[2 + i].wait()
        hub += dot(hub_hot[:, at], feat_ref[at, :])
        slot += dot(slot_hot[:, at], feat_ref[at, :])
    spread(hub, slot, out_ref)


def pick(packet, feats, hub_row, slot_row, flops):
    return pl.pallas_call(
        pick_body,
        out_shape=(packet,)
        + tuple(jax.ShapeDtypeStruct((x.shape[1], feats.shape[0]), BF16) for x in (hub_row, slot_row)),
        in_specs=[pl.BlockSpec(memory_space=pl.ANY)] * 3,
        out_specs=(VM, VM, VM),
        scratch_shapes=[pltpu.VMEM(x.shape, x.dtype) for x in (feats, hub_row, slot_row)]
        + [pltpu.SemaphoreType.DMA((PIECES + 2,))],
        compiler_params=pltpu.CompilerParams(vmem_limit_bytes=16 * MIB),
        cost_estimate=pl.CostEstimate(flops=flops, bytes_accessed=0, transcendentals=0),
    )(*(pltpu.with_memory_space_constraint(x, pltpu.HBM) for x in (feats, hub_row, slot_row)))


def pick_top_body(part_ref, away_ref, hub_hot, slot_hot, hub_ref, slot_ref):
    values = (part_ref[...] + away_ref[...]).astype(BF16)
    top = pl.ds(0, values.shape[0])
    hub_ref[...] = dot(hub_hot[:, top], values)
    slot_ref[...] = dot(slot_hot[:, top], values)


def pick_rest_body(part_ref, away_ref, hub_hot, slot_hot, hub_ref, slot_ref, out_ref):
    values = (part_ref[...] + away_ref[...]).astype(BF16)
    count = values.shape[0]
    rest = pl.ds(hub_hot.shape[1] - count, count)
    hub = hub_ref[...] + dot(hub_hot[:, rest], values)
    slot = slot_ref[...] + dot(slot_hot[:, rest], values)
    spread(hub, slot, out_ref)


def split(got_ref, hubs):
    peers, rows, width = got_ref.shape
    hub = got_ref[:, :hubs, :].reshape(peers * hubs, width)
    slot = got_ref[:, hubs:, :].astype(F32).reshape(peers * (rows - hubs), width).astype(BF16)
    return hub, slot


def first_body(hubs, start, got_ref, hub_mat, sparse_mat, part_ref):
    hub, slot = split(got_ref, hubs)
    for i in range(part_ref.shape[0] // STEP1):
        at = pl.ds(start + i * STEP1, STEP1)
        part_ref[pl.ds(i * STEP1, STEP1), :] = dot(hub_mat[at, :], hub) + dot(sparse_mat[at, :], slot)


def second_rows(step, start, part_ref, hid_hub, hid_slot, hub_mat, sparse_mat):
    for i in range(part_ref.shape[0] // step):
        at = pl.ds(i * step, step)
        src = pl.ds(pl.multiple_of(start + i * step, step), step)
        part_ref[at, :] = dot(hub_mat[src, :], hid_hub[...]) + dot(sparse_mat[src, :], hid_slot[...])


def away_body(hubs, step, got_ref, w_ref, hub_mat, sparse_mat, part_ref, hid_hub, hid_slot):
    hub, slot = split(got_ref, hubs)
    hid_hub[...] = jnp.maximum(dot(hub, w_ref[...]), 0.0).astype(BF16)
    hid_slot[...] = jnp.maximum(dot(slot, w_ref[...]), 0.0).astype(BF16)
    start = (1 - lax.axis_index("rep")) * part_ref.shape[0]
    second_rows(step, start, part_ref, hid_hub, hid_slot, hub_mat, sparse_mat)


def own_body(step, hid_hub, hid_slot, hub_mat, sparse_mat, part_ref):
    start = lax.axis_index("rep") * part_ref.shape[0]
    second_rows(step, start, part_ref, hid_hub, hid_slot, hub_mat, sparse_mat)


def score_body(scale, part_ref, away_ref, w_ref, label_ref, logit_ref, dsec_ref, grad_ref):
    second = (part_ref[...] + away_ref[...]).astype(BF16)
    scores = dot_t(w_ref[...], second)
    logit_ref[...] = scores.astype(BF16)
    top = jnp.max(scores, axis=0, keepdims=True)
    expo = jnp.exp(scores - top)
    probs = expo / jnp.sum(expo, axis=0, keepdims=True)
    hot = label_ref[...] == lax.broadcasted_iota(jnp.int32, scores.shape, 0)
    dscore = (probs - hot.astype(F32)) * scale
    high = dscore.astype(BF16)
    low = (dscore - high.astype(F32)).astype(BF16)
    grad_ref[...] = dot(high, second) + dot(low, second)
    dsec_ref[...] = lax.dot_general(
        w_ref[...], high, (((0,), (0,)), ((), ())), preferred_element_type=F32
    ).astype(BF16)


def back_own_body(step, dsec_ref, hub_mat, sparse_mat, hub_out, slot_out):
    half = dsec_ref.shape[1]
    src = pl.ds(pl.multiple_of(lax.axis_index("rep") * half, half), half)
    slot_out[...] = dot(dsec_ref[...], sparse_mat[src, :])

    @pl.loop(0, hub_mat.shape[1] // step)
    def _(i):
        at = pl.ds(pl.multiple_of(i * step, step), step)
        hub_out[:, at] = dot(dsec_ref[...], hub_mat[src, at])


def back_away_body(
    hubs, step, hub_own, slot_own, grad_ref, dsec_ref, got_ref, hid_hub, hid_slot, hub_mat, sparse_mat, out_ref, acc_ref
):
    half = dsec_ref.shape[1]
    src = pl.ds(pl.multiple_of((1 - lax.axis_index("rep")) * half, half), half)
    peers, rows, width = got_ref.shape

    def term(cols, mat, own, hid):
        grad = jnp.where(hid.astype(F32).T > 0, dot(dsec_ref[...], mat) + own, 0.0).astype(BF16)
        return dot(grad, cols)

    slot = got_ref[:, hubs:, :].astype(F32).reshape(peers * (rows - hubs), width).astype(BF16)
    acc_ref[...] = term(slot, sparse_mat[src, :], slot_own[...], hid_slot[...])
    group = step // hubs

    total = 0.0
    for i in range(hub_mat.shape[1] // step):
        at = pl.ds(i * step, step)
        cols = got_ref[pl.ds(i * group, group), :hubs, :].reshape(step, width)
        total += term(cols, hub_mat[src, at], hub_own[:, at], hid_hub[at, :])
    acc_ref[...] += total

    classes = grad_ref.shape[0]
    rest = out_ref.shape[0] * out_ref.shape[1] - width - classes
    flat = jnp.concatenate([acc_ref[...].T, grad_ref[...], jnp.zeros((rest, out_ref.shape[2]), F32)], axis=0)
    out_ref[...] = flat.reshape(out_ref.shape).astype(BF16)


def fold_body(got_ref, out_ref):
    total = jnp.sum(got_ref[...].astype(F32), axis=0).astype(BF16).astype(F32)
    out_ref[...] = jnp.broadcast_to(total[None], out_ref.shape).astype(BF16)


def parts_body(got_ref, in_ref, out_ref):
    peers, rows, width = got_ref.shape
    whole = got_ref[...].astype(F32).reshape(peers * rows, width)
    first, second = in_ref.shape[0], out_ref.shape[0]
    in_ref[...] = whole[:first]
    out_ref[...] = whole[first : first + second]


def on_device(node_feats, w_in, w_out, labels, hub_rows, send_rows, adj_hub, adj_sparse):
    nrows = lax.axis_size(ROWS)
    slab, width = node_feats.shape
    half = slab // lax.axis_size("rep")
    hid, classes = w_out.shape
    hubs = hub_rows.shape[2]
    slots = send_rows.shape[2] // nrows
    hub_cols, slot_cols = nrows * hubs, nrows * slots
    hub_row = hub_rows.reshape(1, hubs)
    slot_row = send_rows.reshape(1, slot_cols)
    hub_mat = pltpu.with_memory_space_constraint(adj_hub.reshape(slab, hub_cols), pltpu.VMEM)
    sparse_mat = pltpu.with_memory_space_constraint(adj_sparse.reshape(slab, slot_cols), pltpu.VMEM)
    shape = jax.ShapeDtypeStruct
    packet = shape((nrows, hubs + slots, width), BF16)
    products = 2 * slab * (hub_cols + slot_cols)

    def exchange(x, axes=ROWS):
        return lax.all_to_all(x, axes, split_axis=0, concat_axis=0, tiled=True)

    def swap(x):
        return lax.ppermute(x, "rep", SWAP)

    sent, hub_hot, slot_hot = pick(packet, node_feats, hub_row, slot_row, products * 256)
    got = exchange(sent)

    def first_rows(start, rows):
        return call(
            functools.partial(first_body, hubs, start), shape((rows, width), F32), got, hub_mat, sparse_mat,
            flops=products * rows // slab * width * 2,
        )

    top = slab * TOP // 8
    part = first_rows(0, top)
    away = swap(part)
    part_rest = first_rows(top, slab - top)
    away_rest = swap(part_rest)
    hub_some, slot_some = call(
        pick_top_body, (shape((hubs, width), F32), shape((slot_cols, width), F32)), part, away, hub_hot, slot_hot,
        flops=2 * (hubs + slot_cols) * slab * width,
    )
    got = exchange(call(pick_rest_body, packet, part_rest, away_rest, hub_hot, slot_hot, hub_some, slot_some))
    part, hid_hub, hid_slot = call(
        functools.partial(away_body, hubs, STEP2),
        (shape((half, hid), F32), shape((hub_cols, hid), BF16), shape((slot_cols, hid), BF16)),
        got, w_in, hub_mat, sparse_mat,
        flops=products * hid // 2,
    )
    away = swap(part)
    part = call(
        functools.partial(own_body, STEP1), shape((half, hid), F32), hid_hub, hid_slot, hub_mat, sparse_mat,
        flops=products * hid // 2,
    )
    scale = float(1.0 / (slab * nrows) ** 0.5)
    logits, dsec, grad_out = call(
        functools.partial(score_body, scale),
        (shape((classes, half), BF16), shape((hid, half), BF16), shape((classes, hid), F32)),
        part, away, w_out.T, labels.reshape(1, half),
    )
    oth = swap(dsec)
    hub_own, slot_own = call(
        functools.partial(back_own_body, STEP3), (shape((hid, hub_cols), F32), shape((hid, slot_cols), F32)),
        dsec, hub_mat, sparse_mat,
        flops=products * hid // 2,
    )
    count = width + classes
    near, far = lax.axis_size(NEAR), lax.axis_size(FAR)
    share = -(-count // (8 * near)) * 8
    flat = call(
        functools.partial(back_away_body, hubs, STEP4), shape((near, share, hid), BF16),
        hub_own, slot_own, grad_out, oth, got, hid_hub, hid_slot, hub_mat, sparse_mat,
        scratch=[pltpu.VMEM((hid, width), F32)], flops=products * hid // 2,
    )
    piece = call(fold_body, shape((far, share, hid), BF16), exchange(flat, NEAR))
    whole = exchange(call(fold_body, shape((near, share, hid), BF16), exchange(piece, FAR)), NEAR)
    grad_in, grad_out = call(parts_body, (shape((width, hid), F32), shape((classes, hid), F32)), whole)
    return (logits.T, grad_in, grad_out.T)


def solution(mesh):
    rows, cores = mesh.devices.shape
    side = round(rows ** (1 / 3))
    cube = Mesh(mesh.devices.reshape(-1, side, side, cores), ("z", "x", "y", "rep"))
    return jax.shard_map(
        on_device,
        mesh=cube,
        in_specs=(
            P(ROWS, None),
            P(),
            P(),
            P((*ROWS, "rep")),
            P(ROWS, "rep", None),
            P(ROWS, "rep", None),
            P(ROWS, "rep", None),
            P(ROWS, "rep", None),
        ),
        out_specs=(P((*ROWS, "rep"), None), P(), P()),
        check_vma=False,
    )
```
